256 devices in a mesh: band: 64 (over z, y, core), lev: 4 (over x).
Axes of the slice: x: 4, y: 4, z: 8, core: 2. Of those that a mesh axis runs over, the one named last changes fastest.
Arguments:
- winds: float32 [3, 4, 2097152], P(None, 'lev', 'band'), may hold values from -6 to 6
- remap_w: float32 [4, 64, 4096], P(None, 'band'), may hold values from 0.1 to 1
- remap_col: int32 [4, 64, 4096], P(None, 'band'), may hold values from 0 to 1535
- block_pick: int32 [64, 768], replicated, may hold values from 0 to 255
- cycle_ids: int32 [64], P('band'), may hold values from 1024 to 3072
- wave_ids: int32 [2048], replicated, may hold values from 0 to 2047, each once
- legendre_a: bfloat16 [2048, 64, 2048], P(('band', 'lev')), may hold values from -0.01171875 to 0.01171875
- legendre_b: bfloat16 [2048, 64, 2048], P(('band', 'lev')), may hold values from -0.01171875 to 0.01171875
Outputs:
- divergence: float32 [2, 4, 2048, 2048], P(None, None, ('band', 'lev'))
- vorticity: float32 [2, 4, 2048, 2048], P(None, None, ('band', 'lev'))
The draws below stay inside these ranges and needn't reach their ends.
Inputs may be any that keep to these rules, and one draw needn't show every extreme that they name: `block_pick`: block indices within one column shard. `remap_col`: offsets within the 12 picked blocks of one source column shard. `cycle_ids`: Equatorial-belt cycle numbers. `wave_ids`: each wavenumber below 2048 once.
All inputs are finite; a program needn't handle non-finite values.
Results may differ from the reference program's by a relative error of at most 0.0029.
Values may be sent and summed in bfloat16 or wider, within the bound.
A program may use at most 192 MiB of HBM per device.

```python
import math
import jax
import jax.numpy as jnp
from jax import lax

NSIDE = 1024
NPHI = 4096
M = 2048
L = 2048
K = 4
BLK = 128
PER = 12
SB_DEV = 256
CYCLE_DEV = 1
LEVELS = 4
CYCLES = 64
COLS = 2097152
N_BAND = 64


def place_ends(array, own_key, smallest, largest):
    longest = array.shape.index(max(array.shape))
    spots = []
    for shift in (0, 1):
        where = [jax.random.randint(jax.random.fold_in(own_key, axis), (), 0, length) for axis, length in enumerate(array.shape)]
        where[longest] = (where[longest] + shift) % array.shape[longest]
        spots.append(tuple(where))
    return array.at[spots[0]].set(smallest).at[spots[1]].set(largest)


def steps_of(own_key, dims, shards, low, top_value):
    factor_of = 1.0
    for dim, shards_of in shards:
        steps = jax.random.uniform(jax.random.fold_in(jax.random.fold_in(own_key, 6), dim), (shards_of,), jnp.float32, low / len(shards), top_value / len(shards))
        factor_of = factor_of * jnp.repeat(jnp.exp(steps), dims[dim] // shards_of).reshape((-1,) + (1,) * (len(dims) - 1 - dim))
    return factor_of


def noise(rng, dims, scale, bound, split=(), kind=jnp.bfloat16):
    factor_of = steps_of(rng, dims, split, -0.22, 0.18) if split else 1.0
    array = jax.random.normal(rng, dims, jnp.float32) * scale * factor_of
    return jnp.minimum(jnp.maximum(array, -bound), bound).astype(kind)


def setup_inputs(seed: int = 0) -> dict:
    key_list = jax.random.split(jax.random.key(seed), 9)
    return {
        "winds": noise(key_list[0], (3, LEVELS, COLS), 1.0, 6.0, ((1, 4), (2, 64)), jnp.float32),
        "remap_w": jnp.clip(jnp.exp(math.log(1.0) - 2.3025851 * jax.random.uniform(key_list[1], (K, CYCLES, NPHI), jnp.float32) ** steps_of(key_list[1], (K, CYCLES, NPHI), ((1, 64),), -0.2, 0.2)), 0.1, 1.0),
        "remap_col": place_ends(jax.random.randint(key_list[2], (K, CYCLES, NPHI), 0, PER * BLK), jax.random.fold_in(key_list[2], 1), 0, (PER * BLK) - 1).astype(jnp.int32),
        "block_pick": place_ends(jax.random.randint(key_list[3], (N_BAND, N_BAND * PER), 0, SB_DEV), jax.random.fold_in(key_list[3], 1), 0, SB_DEV - 1).astype(jnp.int32),
        "cycle_ids": place_ends(jax.random.randint(key_list[4], (CYCLES,), NSIDE, 3 * NSIDE + 1), jax.random.fold_in(key_list[4], 1), NSIDE, 3 * NSIDE).astype(jnp.int32),
        "wave_ids": jax.random.permutation(key_list[5], M).astype(jnp.int32),
        "legendre_a": noise(key_list[6], (M, CYCLES, L), (CYCLES * NPHI) ** -0.5, 0.01171875, ((0, 256),)),
        "legendre_b": noise(key_list[7], (M, CYCLES, L), (CYCLES * NPHI) ** -0.5, 0.01171875, ((0, 256),)),
    }


def geometry(cycle_number, nside):
    cycle_float = cycle_number.astype(jnp.float32)
    cos_theta = 4.0 / 3.0 - 2.0 * cycle_float / (3.0 * nside)
    sin_theta = jnp.sqrt(1.0 - cos_theta * cos_theta)
    half_shift = ((cycle_number - nside + 1) % 2).astype(jnp.float32)
    return (cos_theta, sin_theta, half_shift)

def reference(winds, remap_w, remap_col, block_pick, cycle_ids, wave_ids, legendre_a, legendre_b):
    cycle_slot = jnp.arange(CYCLES, dtype=jnp.int32)[:, None]
    position = jnp.arange(NPHI, dtype=jnp.int32)[None, :]
    target = cycle_slot // CYCLE_DEV
    pixel = cycle_slot % CYCLE_DEV * NPHI + position
    source = pixel % N_BAND
    picked = block_pick[target[None], source[None] * PER + remap_col // BLK]
    column = source[None] * (SB_DEV * BLK) + picked * BLK + remap_col % BLK
    sampled = winds[:, :, column]
    cartesian = lax.optimization_barrier(jnp.sum(sampled * remap_w[None, None], axis=2))
    cos_theta, sin_theta, half_shift = geometry(cycle_ids, NSIDE)
    spacing = math.pi / (2.0 * NSIDE)
    azimuth = spacing * (position.astype(jnp.float32) + 1.0 - 0.5 * half_shift[:, None])
    cos_phi = jnp.cos(azimuth)
    sin_phi = jnp.sin(azimuth)
    east = -sin_phi * cartesian[0] + cos_phi * cartesian[1]
    north = -cos_theta[:, None] * (cos_phi * cartesian[0] + sin_phi * cartesian[1]) + sin_theta[:, None] * cartesian[2]
    spectra = jnp.fft.rfft(jnp.stack([east, north]), axis=-1)[..., :M]
    raw_real = jnp.real(spectra).astype(jnp.float32)
    raw_imag = jnp.imag(spectra).astype(jnp.float32)
    start = spacing * (1.0 - 0.5 * half_shift)
    angle = start[:, None] * jnp.arange(M, dtype=jnp.int32).astype(jnp.float32)[None, :]
    cos_rot = jnp.cos(angle)
    sin_rot = jnp.sin(angle)
    rot_real = raw_real * cos_rot + raw_imag * sin_rot
    rot_imag = raw_imag * cos_rot - raw_real * sin_rot
    modes = jnp.stack([rot_real[0], rot_imag[0], rot_real[1], rot_imag[1]], axis=1).astype(jnp.bfloat16)
    chosen = jnp.take(modes, wave_ids, axis=3)
    slot_rows = jnp.transpose(chosen, (3, 0, 1, 2)).reshape(M, LEVELS * 4, CYCLES)
    degree = jnp.arange(L, dtype=jnp.int32)

    def one_slot(item):
        mode_rows, table_a, table_b, wavenumber = item
        part_a = jnp.dot(mode_rows, table_a, preferred_element_type=jnp.float32).reshape(LEVELS, 4, L)
        part_b = jnp.dot(mode_rows, table_b, preferred_element_type=jnp.float32).reshape(LEVELS, 4, L)
        upper = (degree >= wavenumber)[None, :]
        div_real = jnp.where(upper, -part_a[:, 1] - part_b[:, 2], 0.0)
        div_imag = jnp.where(upper, part_a[:, 0] - part_b[:, 3], 0.0)
        vort_real = jnp.where(upper, -part_a[:, 3] + part_b[:, 0], 0.0)
        vort_imag = jnp.where(upper, part_a[:, 2] + part_b[:, 1], 0.0)
        return (jnp.stack([div_real, div_imag]), jnp.stack([vort_real, vort_imag]))
    div_all, vort_all = lax.map(one_slot, (slot_rows, legendre_a, legendre_b, wave_ids))
    return (jnp.transpose(div_all, (1, 2, 0, 3)), jnp.transpose(vort_all, (1, 2, 0, 3)))
```

```python
import functools
import math

import jax
import jax.numpy as jnp
import numpy as np
from jax import lax
from jax.experimental import pallas as pl
from jax.experimental.pallas import tpu as pltpu
from jax.sharding import PartitionSpec as P

NSIDE = 1024
NPHI = 4096
M = 2048
BLK = 128
PER = 12
TAPS = 4
LANES = 128

f32 = jnp.float32
bf16 = jnp.bfloat16


def split(table):
    table = np.asarray(table, np.float32)
    high = table.astype(jnp.bfloat16)
    low = (table - high.astype(np.float32)).astype(jnp.bfloat16)
    return high, low


@functools.cache
def tables(band):
    rho = np.arange(2 * band)
    n = (rho % 2) * band + rho // 2
    b = np.arange(NPHI // (2 * band))
    mu = np.arange(LANES)
    m1 = np.arange(M // LANES)
    turn = 2.0 * np.pi / NPHI
    coef, twiddle, outer_hi, outer_lo = [], [], [], []
    for half in (0, 1):
        delta = 1.0 - 0.5 * half
        azimuth = turn * (2 * band * b[None, :] + n[:, None] + delta)
        zero = np.zeros_like(azimuth)
        cos, sin = np.cos(azimuth), np.sin(azimuth)
        coef.append(np.stack([np.concatenate([-sin, cos, zero, zero], 1), np.concatenate([cos, sin, zero, zero], 1)]))
        phi = turn * mu[None, :] * (n[:, None] + delta)
        twiddle.append(np.stack([np.cos(phi), np.sin(phi)]))
        psi = turn * LANES * m1[:, None] * (n[None, :] + delta)
        full = np.concatenate(
            [np.concatenate([np.cos(psi), np.sin(psi)], 1), np.concatenate([-np.sin(psi), np.cos(psi)], 1)], 0
        )
        high, low = split(full)
        outer_hi.append(high)
        outer_lo.append(low)
    angle = 2.0 * np.pi / b.size * (b[:, None] * mu[None, :])
    inner = np.tile(np.concatenate([np.cos(angle), -np.sin(angle)], 1), (4, 1))
    inner_hi, inner_lo = split(inner)
    return (
        np.stack(coef).astype(np.float32),
        np.stack(twiddle).astype(np.float32),
        np.stack([inner_hi, inner_lo]),
        np.stack([np.stack(outer_hi), np.stack(outer_lo)]),
    )


def dot(a, b):
    return jnp.dot(a, b, preferred_element_type=f32)


def high_low(x):
    high = x.astype(bf16)
    return high, (x - high.astype(f32)).astype(bf16)


def take(x, index):
    return jnp.take_along_axis(x, index, axis=1, mode="promise_in_bounds")


def modes_kernel(
    band,
    lev,
    cycle_ref,
    winds_hbm,
    weight_hbm,
    column_hbm,
    pick_hbm,
    wave_hbm,
    coef_hbm,
    twiddle_hbm,
    inner_hbm,
    outer_hbm,
    out_ref,
    winds,
    weight,
    column,
    pick,
    wave,
    coef,
    twiddle,
    inner,
    outer,
    table,
    request_out,
    request_in,
    reply_out,
    reply_in,
    spectrum,
    rows_out,
    rows_in,
    turned,
    levels_in,
    local_sem,
    send_sem,
    recv_sem,
):
    me = lax.axis_index("band")
    my_lev = lax.axis_index("lev")
    window = jnp.minimum(me * PER // LANES, PER * band // LANES - 2)
    pick_at = me * PER - window * LANES
    loads = [
        pltpu.make_async_copy(source, target, local_sem.at[i])
        for i, (source, target) in enumerate(
            (
                (column_hbm, column),
                (weight_hbm, weight),
                (winds_hbm, winds),
                (pick_hbm.at[:, pl.ds(pl.multiple_of(window * LANES, LANES), 2 * LANES)], pick),
                (coef_hbm, coef),
                (twiddle_hbm, twiddle),
                (inner_hbm, inner),
                (outer_hbm, outer),
                (wave_hbm, wave),
            )
        )
    ]
    for load in loads:
        load.start()

    def to_band(source, target, other, phase):
        return pltpu.make_async_remote_copy(
            src_ref=source,
            dst_ref=target,
            send_sem=send_sem.at[phase],
            recv_sem=recv_sem.at[phase],
            device_id=(other, my_lev),
            device_id_type=pl.DeviceIdType.MESH,
        )

    loads[0].wait()
    loads[1].wait()
    turned_column = column[...].astype(f32).T
    turned_weight = weight[...].T
    for h in range(2):
        request_out[pl.ds(h, band, stride=4), :] = turned_column[h * band : (h + 1) * band]
        request_out[pl.ds(2 + h, band, stride=4), :] = turned_weight[h * band : (h + 1) * band]
    mine = pltpu.make_async_copy(
        request_out.at[pl.ds(4 * me, 4)], request_in.at[pl.ds(4 * me, 4)], recv_sem.at[0]
    )
    mine.start()

    def send_request(i, carry):
        other = lax.rem(me + i, band)
        to_band(request_out.at[pl.ds(4 * other, 4)], request_in.at[pl.ds(4 * me, 4)], other, 0).start()
        return carry

    lax.fori_loop(1, band, send_request, 0)

    loads[2].wait()
    blocks = winds.shape[0] // 3
    for a in range(3):
        part = winds[pl.ds(a * blocks, blocks), :]
        table[:, a, :] = part
        table[:, 4 + a, :] = part
    loads[3].wait()
    pltpu.make_async_copy(request_in, request_in, recv_sem.at[0]).wait()

    sub = lax.broadcasted_iota(jnp.int32, (8, LANES), 0)
    lane = lax.broadcasted_iota(jnp.int32, (8, LANES), 1)
    upper = sub < 4
    own_group = (lane >> 5) == (sub & 3)

    def weigh(other):
        rows = [jnp.broadcast_to(request_in[pl.ds(4 * other + k, 1), :], (8, LANES)) for k in range(4)]
        where = jnp.where(upper, rows[0], rows[1]).astype(jnp.int32)
        scale = jnp.where(upper, rows[2], rows[3])
        within, block = where & (BLK - 1), where >> 7
        total = jnp.zeros((8, LANES), f32)
        for c in range(PER):
            piece = table[pick[other, pick_at + c]]
            total = jnp.where(block == c, take(piece, within), total)
        total = total * scale
        total = total + pltpu.roll(total, 64, 1)
        total = total + pltpu.roll(total, 32, 1)
        total = jnp.where(own_group, total, 0.0)
        total = total + pltpu.roll(total, 1, 0)
        total = total + pltpu.roll(total, 2, 0)
        reply_out[pl.ds(2 * other, 1), :] = total[3:4]
        reply_out[pl.ds(2 * other + 1, 1), :] = total[7:8]

    weigh(me)
    mine = pltpu.make_async_copy(
        reply_out.at[pl.ds(2 * me, 2)], reply_in.at[pl.ds(2 * me, 2)], recv_sem.at[1]
    )
    mine.start()
    group = 7

    def send_reply(i, carry):
        for u in range(group):
            weigh(lax.rem(me + 1 + i * group + u, band))
        for u in range(group):
            other = lax.rem(me + 1 + i * group + u, band)
            to_band(reply_out.at[pl.ds(2 * other, 2)], reply_in.at[pl.ds(2 * me, 2)], other, 1).start()
        return carry

    lax.fori_loop(0, (band - 1) // group, send_reply, 0)
    for load in loads[4:]:
        load.wait()
    pltpu.make_async_copy(reply_in, reply_in, recv_sem.at[1]).wait()

    number = cycle_ref[0]
    odd = (jnp.full((2 * band, LANES), number, jnp.int32) & 1) == 1
    odd_thin = (jnp.full((2 * M // LANES, 4 * band), number, jnp.int32) & 1) == 1

    def by_parity(table, *at):
        return jnp.where(odd, table[(0, *at)], table[(1, *at)])

    cos_theta = 4.0 / 3.0 - 2.0 * jnp.full((2 * band, LANES), number, jnp.int32).astype(f32) / (3.0 * NSIDE)
    sin_theta = jnp.sqrt(1.0 - cos_theta * cos_theta)
    component = lax.broadcasted_iota(jnp.int32, (2 * band, LANES), 1) >> 5
    samples = reply_in[...]
    east = samples * by_parity(coef, 0)
    north = samples * jnp.where(component == 2, sin_theta, -cos_theta * by_parity(coef, 1))
    high, low = high_low(jnp.concatenate([east, north], 0))
    section = dot(high, inner[0]) + dot(low, inner[0]) + dot(high, inner[1])
    cos, sin = by_parity(twiddle, 0), by_parity(twiddle, 1)
    cos, sin = jnp.concatenate([cos, cos], 0), jnp.concatenate([sin, sin], 0)
    real, imag = section[:, :LANES], section[:, LANES:]
    real, imag = real * cos + imag * sin, imag * cos - real * sin
    n = 2 * band
    high, low = high_low(
        jnp.concatenate(
            [jnp.concatenate([real[:n], real[n:]], 1), jnp.concatenate([imag[:n], imag[n:]], 1)], 0
        )
    )
    outer_hi = jnp.where(odd_thin, outer[0, 0], outer[0, 1])
    outer_lo = jnp.where(odd_thin, outer[1, 0], outer[1, 1])
    full = dot(outer_hi, high) + dot(outer_hi, low) + dot(outer_lo, high)
    full = full.astype(bf16).astype(f32)
    rows = M // LANES
    for f, (r, c) in enumerate(((0, 0), (1, 0), (0, 1), (1, 1))):
        spectrum[pl.ds(f * rows, rows), :] = full[r * rows : (r + 1) * rows, c * LANES : (c + 1) * LANES]

    wave_row, wave_lane = wave[...] >> 7, wave[...] & (LANES - 1)
    field = (lane >> 3) & 3
    spot = (lane >> 5) * 8 + (lane & 7)
    for h in range(rows // 8):
        row_of, lane_of = wave_row[8 * h : 8 * h + 8], wave_lane[8 * h : 8 * h + 8]
        ordered = []
        for f in range(4):
            picked = jnp.zeros((8, LANES), f32)
            for r in range(rows):
                source = jnp.broadcast_to(spectrum[pl.ds(f * rows + r, 1), :], (8, LANES))
                picked = jnp.where(row_of == r, take(source, lane_of), picked)
            ordered.append(picked)
        for b in range(4):
            packed = jnp.zeros((8, LANES), f32)
            for f in range(4):
                packed = jnp.where(field == f, take(ordered[f], spot + 32 * b), packed)
            rows_out[pl.ds(b * rows + 8 * h, 8), :] = packed

    def row_for(other):
        return lax.rem(other, 4) * rows + other // 4

    mine = pltpu.make_async_copy(rows_out.at[pl.ds(row_for(me), 1)], rows_in.at[pl.ds(me, 1)], recv_sem.at[2])
    mine.start()

    def send_rows(i, carry):
        other = lax.rem(me + i, band)
        to_band(rows_out.at[pl.ds(row_for(other), 1)], rows_in.at[pl.ds(me, 1)], other, 2).start()
        return carry

    lax.fori_loop(1, band, send_rows, 0)
    pltpu.make_async_copy(rows_in, rows_in, recv_sem.at[2]).wait()

    arrived = rows_in[...]
    turned[...] = jnp.concatenate([arrived, arrived], 0).T.reshape(turned.shape)
    mine = pltpu.make_async_copy(turned.at[my_lev], levels_in.at[:, my_lev], recv_sem.at[3])
    mine.start()

    def to_level(other):
        return pltpu.make_async_remote_copy(
            src_ref=turned.at[other],
            dst_ref=levels_in.at[:, my_lev],
            send_sem=send_sem.at[3],
            recv_sem=recv_sem.at[3],
            device_id=(me, other),
            device_id_type=pl.DeviceIdType.MESH,
        )

    for i in range(1, lev):
        to_level(lax.rem(my_lev + i, lev)).start()
    pltpu.make_async_copy(levels_in, levels_in, recv_sem.at[3]).wait()

    first = lax.broadcasted_iota(jnp.int32, (8, LANES), 1) < band
    sign_a, sign_b = (-1.0, 1.0, -1.0, 1.0), (-1.0, -1.0, 1.0, 1.0)
    for o in range(4):
        for v in range(lev):
            out_ref[pl.ds((o * lev + v) * 8, 8), :] = jnp.where(
                first, sign_a[o] * levels_in[o ^ 1, v], sign_b[o] * levels_in[o ^ 2, v]
            )

    pltpu.make_async_copy(request_out.at[pl.ds(0, 4 * (band - 1))], request_out.at[pl.ds(0, 4 * (band - 1))], send_sem.at[0]).wait()
    pltpu.make_async_copy(reply_out.at[pl.ds(0, 2 * (band - 1))], reply_out.at[pl.ds(0, 2 * (band - 1))], send_sem.at[1]).wait()
    pltpu.make_async_copy(rows_out.at[pl.ds(0, band - 1)], rows_out.at[pl.ds(0, band - 1)], send_sem.at[2]).wait()
    pltpu.make_async_copy(turned.at[pl.ds(0, lev - 1)], turned.at[pl.ds(0, lev - 1)], send_sem.at[3]).wait()


def legendre_kernel(owned, wave_ref, left_ref, a_ref, b_ref, div_ref, vort_ref):
    me = lax.axis_index("band") * lax.axis_size("lev") + lax.axis_index("lev")
    width = a_ref.shape[2]
    rows = left_ref.shape[0]
    left = left_ref[...]
    slot = lax.broadcasted_iota(jnp.int32, left.shape, 0) % owned
    pieces = [jnp.where(slot == i, left, 0.0).astype(bf16) for i in range(owned)]
    total = jnp.zeros((rows, width), f32)
    for i in range(0, owned, 2):
        right = jnp.concatenate([a_ref[i], b_ref[i], a_ref[i + 1], b_ref[i + 1]], 0)
        total = total + dot(jnp.concatenate([pieces[i], pieces[i + 1]], 1), right)
    lowest = jnp.zeros((owned, width), jnp.int32)
    row = lax.broadcasted_iota(jnp.int32, lowest.shape, 0)
    for i in range(owned):
        lowest = jnp.where(row == i, wave_ref[me * owned + i], lowest)
    degree = pl.program_id(0) * width + lax.broadcasted_iota(jnp.int32, lowest.shape, 1)
    keep = degree >= lowest
    half = rows // 2
    for r in range(0, half, owned):
        div_ref[r : r + owned] = jnp.where(keep, total[r : r + owned], 0.0)
        vort_ref[r : r + owned] = jnp.where(keep, total[half + r : half + r + owned], 0.0)


def local(winds, remap_w, remap_col, block_pick, cycle_ids, wave_ids, legendre_a, legendre_b):
    band, lev = lax.axis_size("band"), lax.axis_size("lev")
    coef, twiddle, inner, outer = tables(band)
    columns = winds.shape[2]
    owned, cycles, degrees = legendre_a.shape
    blocks = columns // BLK
    hbm = pl.BlockSpec(memory_space=pltpu.HBM)
    smem = pl.BlockSpec(memory_space=pltpu.SMEM)
    vmem = pl.BlockSpec(memory_space=pltpu.VMEM)
    left = pl.pallas_call(
        functools.partial(modes_kernel, band, lev),
        out_shape=jax.ShapeDtypeStruct((4 * lev * owned, 2 * cycles), f32),
        in_specs=[smem] + [hbm] * 9,
        out_specs=vmem,
        scratch_shapes=[
            pltpu.VMEM((3 * blocks, BLK), f32),
            pltpu.VMEM((2 * band, LANES), f32),
            pltpu.VMEM((2 * band, LANES), jnp.int32),
            pltpu.SMEM((band, 2 * LANES), jnp.int32),
            pltpu.VMEM((M // LANES, LANES), jnp.int32),
            pltpu.VMEM(coef.shape, f32),
            pltpu.VMEM(twiddle.shape, f32),
            pltpu.VMEM(inner.shape, bf16),
            pltpu.VMEM(outer.shape, bf16),
            pltpu.VMEM((blocks, 8, BLK), f32),
            pltpu.VMEM((4 * band, LANES), f32),
            pltpu.VMEM((4 * band, LANES), f32),
            pltpu.VMEM((2 * band, LANES), f32),
            pltpu.VMEM((2 * band, LANES), f32),
            pltpu.VMEM((4 * M // LANES, LANES), f32),
            pltpu.VMEM((band, LANES), f32),
            pltpu.VMEM((band, LANES), f32),
            pltpu.VMEM((lev, 4, owned, LANES), f32),
            pltpu.VMEM((4, lev, owned, LANES), f32),
            pltpu.SemaphoreType.DMA((9,)),
            pltpu.SemaphoreType.DMA((4,)),
            pltpu.SemaphoreType.DMA((4,)),
        ],
        compiler_params=pltpu.CompilerParams(has_side_effects=True, vmem_limit_bytes=60 * 2**20),
        name="modes",
    )(
        cycle_ids,
        winds.reshape(3 * blocks, BLK),
        remap_w.reshape(2 * band, LANES),
        remap_col.reshape(2 * band, LANES),
        block_pick,
        wave_ids.reshape(M // LANES, LANES),
        coef,
        twiddle,
        inner,
        outer,
    )
    width = 512
    shape = jax.ShapeDtypeStruct((2 * lev * owned, degrees), f32)
    divergence, vorticity = pl.pallas_call(
        functools.partial(legendre_kernel, owned),
        grid=(degrees // width,),
        out_shape=(shape, shape),
        in_specs=[
            smem,
            pl.BlockSpec((4 * lev * owned, 2 * cycles), lambda j: (0, 0)),
            pl.BlockSpec((owned, cycles, width), lambda j: (0, 0, j)),
            pl.BlockSpec((owned, cycles, width), lambda j: (0, 0, j)),
        ],
        out_specs=(
            pl.BlockSpec((2 * lev * owned, width), lambda j: (0, j)),
            pl.BlockSpec((2 * lev * owned, width), lambda j: (0, j)),
        ),
        compiler_params=pltpu.CompilerParams(vmem_limit_bytes=60 * 2**20),
        name="legendre",
    )(wave_ids, left, legendre_a, legendre_b)
    whole = (2, lev, owned, degrees)
    return divergence.reshape(whole), vorticity.reshape(whole)


def solution(mesh):
    placed = (
        P(None, "lev", "band"),
        P(None, "band", None),
        P(None, "band", None),
        P(),
        P("band"),
        P(),
        P(("band", "lev"), None, None),
        P(("band", "lev"), None, None),
    )
    return jax.shard_map(
        local,
        mesh=mesh,
        in_specs=placed,
        out_specs=(P(None, None, ("band", "lev"), None), P(None, None, ("band", "lev"), None)),
        check_vma=False,
    )
```

```python
import functools
import math

import jax
import jax.numpy as jnp
import numpy as np
from jax import lax
from jax.experimental import pallas as pl
from jax.experimental.pallas import tpu as pltpu
from jax.sharding import PartitionSpec as P

NSIDE = 1024
NPHI = 4096
M = 2048
BLK = 128
PER = 12
TAPS = 4
LANES = 128

f32 = jnp.float32
bf16 = jnp.bfloat16


def split(table):
    table = np.asarray(table, np.float32)
    high = table.astype(jnp.bfloat16)
    low = (table - high.astype(np.float32)).astype(jnp.bfloat16)
    return high, low


@functools.cache
def tables(band):
    rho = np.arange(2 * band)
    n = (rho % 2) * band + rho // 2
    b = np.arange(NPHI // (2 * band))
    mu = np.arange(LANES)
    m1 = np.arange(M // LANES)
    turn = 2.0 * np.pi / NPHI
    coef, twiddle, outer_hi, outer_lo = [], [], [], []
    for half in (0, 1):
        delta = 1.0 - 0.5 * half
        azimuth = turn * (2 * band * b[None, :] + n[:, None] + delta)
        zero = np.zeros_like(azimuth)
        cos, sin = np.cos(azimuth), np.sin(azimuth)
        coef.append(np.stack([np.concatenate([-sin, cos, zero, zero], 1), np.concatenate([cos, sin, zero, zero], 1)]))
        phi = turn * mu[None, :] * (n[:, None] + delta)
        twiddle.append(np.stack([np.cos(phi), np.sin(phi)]))
        psi = turn * LANES * m1[:, None] * (n[None, :] + delta)
        full = np.concatenate(
            [np.concatenate([np.cos(psi), np.sin(psi)], 1), np.concatenate([-np.sin(psi), np.cos(psi)], 1)], 0
        )
        high, low = split(full)
        outer_hi.append(high)
        outer_lo.append(low)
    angle = 2.0 * np.pi / b.size * (b[:, None] * mu[None, :])
    inner = np.tile(np.concatenate([np.cos(angle), -np.sin(angle)], 1), (4, 1))
    inner_hi, inner_lo = split(inner)
    return (
        np.stack(coef).astype(np.float32),
        np.stack(twiddle).astype(np.float32),
        np.stack([inner_hi, inner_lo]),
        np.stack([np.stack(outer_hi), np.stack(outer_lo)]),
    )


def dot(a, b):
    return jnp.dot(a, b, preferred_element_type=f32)


def high_low(x):
    high = x.astype(bf16)
    return high, (x - high.astype(f32)).astype(bf16)


def take(x, index):
    return jnp.take_along_axis(x, index, axis=1, mode="promise_in_bounds")


def modes_kernel(
    band,
    lev,
    cycle_ref,
    winds_hbm,
    weight_hbm,
    column_hbm,
    pick_hbm,
    wave_hbm,
    coef_hbm,
    twiddle_hbm,
    inner_hbm,
    outer_hbm,
    out_ref,
    winds,
    weight,
    column,
    pick,
    wave,
    coef,
    twiddle,
    inner,
    outer,
    table,
    request_out,
    request_in,
    reply_out,
    reply_in,
    spectrum,
    rows_out,
    rows_in,
    turned,
    levels_in,
    local_sem,
    send_sem,
    recv_sem,
):
    me = lax.axis_index("band")
    my_lev = lax.axis_index("lev")
    barrier = pltpu.get_barrier_semaphore()

    def greet(i, carry):
        other = lax.rem(me + i, band)
        pl.semaphore_signal(barrier, 1, device_id=(other, my_lev), device_id_type=pl.DeviceIdType.MESH)
        return carry

    lax.fori_loop(1, band, greet, 0)
    for i in range(1, lev):
        other = lax.rem(my_lev + i, lev)
        pl.semaphore_signal(barrier, 1, device_id=(me, other), device_id_type=pl.DeviceIdType.MESH)

    window = jnp.minimum(me * PER // LANES, PER * band // LANES - 2)
    pick_at = me * PER - window * LANES
    loads = [
        pltpu.make_async_copy(source, target, local_sem.at[i])
        for i, (source, target) in enumerate(
            (
                (column_hbm, column),
                (weight_hbm, weight),
                (winds_hbm, winds),
                (pick_hbm.at[:, pl.ds(pl.multiple_of(window * LANES, LANES), 2 * LANES)], pick),
                (coef_hbm, coef),
                (twiddle_hbm, twiddle),
                (inner_hbm, inner),
                (outer_hbm, outer),
                (wave_hbm, wave),
            )
        )
    ]
    for load in loads:
        load.start()

    def to_band(source, target, other, phase):
        return pltpu.make_async_remote_copy(
            src_ref=source,
            dst_ref=target,
            send_sem=send_sem.at[phase],
            recv_sem=recv_sem.at[phase],
            device_id=(other, my_lev),
            device_id_type=pl.DeviceIdType.MESH,
        )

    loads[0].wait()
    loads[1].wait()
    turned_column = column[...].astype(f32).T
    turned_weight = weight[...].T
    for h in range(2):
        request_out[pl.ds(h, band, stride=4), :] = turned_column[h * band : (h + 1) * band]
        request_out[pl.ds(2 + h, band, stride=4), :] = turned_weight[h * band : (h + 1) * band]
    loads[2].wait()
    blocks = winds.shape[0] // 3
    for a in range(3):
        part = winds[pl.ds(a * blocks, blocks), :]
        table[:, a, :] = part
        table[:, 4 + a, :] = part
    pl.semaphore_wait(barrier, band - 1 + lev - 1)
    mine = pltpu.make_async_copy(
        request_out.at[pl.ds(4 * me, 4)], request_in.at[pl.ds(4 * me, 4)], recv_sem.at[0]
    )
    mine.start()

    def send_request(i, carry):
        other = lax.rem(me + i, band)
        to_band(request_out.at[pl.ds(4 * other, 4)], request_in.at[pl.ds(4 * me, 4)], other, 0).start()
        return carry

    lax.fori_loop(1, band, send_request, 0)
    loads[3].wait()
    pltpu.make_async_copy(request_in, request_in, recv_sem.at[0]).wait()

    sub = lax.broadcasted_iota(jnp.int32, (8, LANES), 0)
    lane = lax.broadcasted_iota(jnp.int32, (8, LANES), 1)
    upper = sub < 4
    own_group = (lane >> 5) == (sub & 3)

    def weigh(other):
        rows = [jnp.broadcast_to(request_in[pl.ds(4 * other + k, 1), :], (8, LANES)) for k in range(4)]
        where = jnp.where(upper, rows[0], rows[1]).astype(jnp.int32)
        scale = jnp.where(upper, rows[2], rows[3])
        within, block = where & (BLK - 1), where >> 7
        total = jnp.zeros((8, LANES), f32)
        for c in range(PER):
            piece = table[pick[other, pick_at + c]]
            total = jnp.where(block == c, take(piece, within), total)
        total = total * scale
        total = total + pltpu.roll(total, 64, 1)
        total = total + pltpu.roll(total, 32, 1)
        total = jnp.where(own_group, total, 0.0)
        total = total + pltpu.roll(total, 1, 0)
        total = total + pltpu.roll(total, 2, 0)
        reply_out[pl.ds(2 * other, 1), :] = total[3:4]
        reply_out[pl.ds(2 * other + 1, 1), :] = total[7:8]

    weigh(me)
    mine = pltpu.make_async_copy(
        reply_out.at[pl.ds(2 * me, 2)], reply_in.at[pl.ds(2 * me, 2)], recv_sem.at[1]
    )
    mine.start()
    group = 7

    def send_reply(i, carry):
        for u in range(group):
            weigh(lax.rem(me + 1 + i * group + u, band))
        for u in range(group):
            other = lax.rem(me + 1 + i * group + u, band)
            to_band(reply_out.at[pl.ds(2 * other, 2)], reply_in.at[pl.ds(2 * me, 2)], other, 1).start()
        return carry

    lax.fori_loop(0, (band - 1) // group, send_reply, 0)
    for load in loads[4:]:
        load.wait()
    pltpu.make_async_copy(reply_in, reply_in, recv_sem.at[1]).wait()

    number = cycle_ref[0]
    odd = (jnp.full((2 * band, LANES), number, jnp.int32) & 1) == 1
    odd_thin = (jnp.full((2 * M // LANES, 4 * band), number, jnp.int32) & 1) == 1

    def by_parity(table, *at):
        return jnp.where(odd, table[(0, *at)], table[(1, *at)])

    cos_theta = 4.0 / 3.0 - 2.0 * jnp.full((2 * band, LANES), number, jnp.int32).astype(f32) / (3.0 * NSIDE)
    sin_theta = jnp.sqrt(1.0 - cos_theta * cos_theta)
    component = lax.broadcasted_iota(jnp.int32, (2 * band, LANES), 1) >> 5
    samples = reply_in[...]
    east = samples * by_parity(coef, 0)
    north = samples * jnp.where(component == 2, sin_theta, -cos_theta * by_parity(coef, 1))
    high, low = high_low(jnp.concatenate([east, north], 0))
    section = dot(high, inner[0]) + dot(low, inner[0]) + dot(high, inner[1])
    cos, sin = by_parity(twiddle, 0), by_parity(twiddle, 1)
    cos, sin = jnp.concatenate([cos, cos], 0), jnp.concatenate([sin, sin], 0)
    real, imag = section[:, :LANES], section[:, LANES:]
    real, imag = real * cos + imag * sin, imag * cos - real * sin
    n = 2 * band
    high, low = high_low(
        jnp.concatenate(
            [jnp.concatenate([real[:n], real[n:]], 1), jnp.concatenate([imag[:n], imag[n:]], 1)], 0
        )
    )
    outer_hi = jnp.where(odd_thin, outer[0, 0], outer[0, 1])
    outer_lo = jnp.where(odd_thin, outer[1, 0], outer[1, 1])
    full = dot(outer_hi, high) + dot(outer_hi, low) + dot(outer_lo, high)
    full = full.astype(bf16).astype(f32)
    rows = M // LANES
    for f, (r, c) in enumerate(((0, 0), (1, 0), (0, 1), (1, 1))):
        spectrum[pl.ds(f * rows, rows), :] = full[r * rows : (r + 1) * rows, c * LANES : (c + 1) * LANES]

    wave_row, wave_lane = wave[...] >> 7, wave[...] & (LANES - 1)
    field = (lane >> 3) & 3
    spot = (lane >> 5) * 8 + (lane & 7)
    for h in range(rows // 8):
        row_of, lane_of = wave_row[8 * h : 8 * h + 8], wave_lane[8 * h : 8 * h + 8]
        ordered = []
        for f in range(4):
            picked = jnp.zeros((8, LANES), f32)
            for r in range(rows):
                source = jnp.broadcast_to(spectrum[pl.ds(f * rows + r, 1), :], (8, LANES))
                picked = jnp.where(row_of == r, take(source, lane_of), picked)
            ordered.append(picked)
        for b in range(4):
            packed = jnp.zeros((8, LANES), f32)
            for f in range(4):
                packed = jnp.where(field == f, take(ordered[f], spot + 32 * b), packed)
            rows_out[pl.ds(b * rows + 8 * h, 8), :] = packed

    def row_for(other):
        return lax.rem(other, 4) * rows + other // 4

    mine = pltpu.make_async_copy(rows_out.at[pl.ds(row_for(me), 1)], rows_in.at[pl.ds(me, 1)], recv_sem.at[2])
    mine.start()

    def send_rows(i, carry):
        other = lax.rem(me + i, band)
        to_band(rows_out.at[pl.ds(row_for(other), 1)], rows_in.at[pl.ds(me, 1)], other, 2).start()
        return carry

    lax.fori_loop(1, band, send_rows, 0)
    pltpu.make_async_copy(rows_in, rows_in, recv_sem.at[2]).wait()

    arrived = rows_in[...]
    turned[...] = jnp.concatenate([arrived, arrived], 0).T.reshape(turned.shape)
    mine = pltpu.make_async_copy(turned.at[my_lev], levels_in.at[:, my_lev], recv_sem.at[3])
    mine.start()

    def to_level(other):
        return pltpu.make_async_remote_copy(
            src_ref=turned.at[other],
            dst_ref=levels_in.at[:, my_lev],
            send_sem=send_sem.at[3],
            recv_sem=recv_sem.at[3],
            device_id=(me, other),
            device_id_type=pl.DeviceIdType.MESH,
        )

    for i in range(1, lev):
        to_level(lax.rem(my_lev + i, lev)).start()
    pltpu.make_async_copy(levels_in, levels_in, recv_sem.at[3]).wait()

    first = lax.broadcasted_iota(jnp.int32, (8, LANES), 1) < band
    sign_a, sign_b = (-1.0, 1.0, -1.0, 1.0), (-1.0, -1.0, 1.0, 1.0)
    for o in range(4):
        for v in range(lev):
            out_ref[pl.ds((o * lev + v) * 8, 8), :] = jnp.where(
                first, sign_a[o] * levels_in[o ^ 1, v], sign_b[o] * levels_in[o ^ 2, v]
            )

    pltpu.make_async_copy(request_out.at[pl.ds(0, 4 * (band - 1))], request_out.at[pl.ds(0, 4 * (band - 1))], send_sem.at[0]).wait()
    pltpu.make_async_copy(reply_out.at[pl.ds(0, 2 * (band - 1))], reply_out.at[pl.ds(0, 2 * (band - 1))], send_sem.at[1]).wait()
    pltpu.make_async_copy(rows_out.at[pl.ds(0, band - 1)], rows_out.at[pl.ds(0, band - 1)], send_sem.at[2]).wait()
    pltpu.make_async_copy(turned.at[pl.ds(0, lev - 1)], turned.at[pl.ds(0, lev - 1)], send_sem.at[3]).wait()


def legendre_kernel(owned, wave_ref, left_ref, a_ref, b_ref, div_ref, vort_ref):
    me = lax.axis_index("band") * lax.axis_size("lev") + lax.axis_index("lev")
    width = a_ref.shape[2]
    rows = left_ref.shape[0]
    left = left_ref[...]
    slot = lax.broadcasted_iota(jnp.int32, left.shape, 0) % owned
    pieces = [jnp.where(slot == i, left, 0.0).astype(bf16) for i in range(owned)]
    total = jnp.zeros((rows, width), f32)
    for i in range(0, owned, 2):
        right = jnp.concatenate([a_ref[i], b_ref[i], a_ref[i + 1], b_ref[i + 1]], 0)
        total = total + dot(jnp.concatenate([pieces[i], pieces[i + 1]], 1), right)
    lowest = jnp.zeros((owned, width), jnp.int32)
    row = lax.broadcasted_iota(jnp.int32, lowest.shape, 0)
    for i in range(owned):
        lowest = jnp.where(row == i, wave_ref[me * owned + i], lowest)
    degree = pl.program_id(0) * width + lax.broadcasted_iota(jnp.int32, lowest.shape, 1)
    keep = degree >= lowest
    half = rows // 2
    for r in range(0, half, owned):
        div_ref[r : r + owned] = jnp.where(keep, total[r : r + owned], 0.0)
        vort_ref[r : r + owned] = jnp.where(keep, total[half + r : half + r + owned], 0.0)


def local(winds, remap_w, remap_col, block_pick, cycle_ids, wave_ids, legendre_a, legendre_b):
    band, lev = lax.axis_size("band"), lax.axis_size("lev")
    coef, twiddle, inner, outer = tables(band)
    columns = winds.shape[2]
    owned, cycles, degrees = legendre_a.shape
    blocks = columns // BLK
    hbm = pl.BlockSpec(memory_space=pltpu.HBM)
    smem = pl.BlockSpec(memory_space=pltpu.SMEM)
    vmem = pl.BlockSpec(memory_space=pltpu.VMEM)
    left = pl.pallas_call(
        functools.partial(modes_kernel, band, lev),
        out_shape=jax.ShapeDtypeStruct((4 * lev * owned, 2 * cycles), f32),
        in_specs=[smem] + [hbm] * 9,
        out_specs=vmem,
        scratch_shapes=[
            pltpu.VMEM((3 * blocks, BLK), f32),
            pltpu.VMEM((2 * band, LANES), f32),
            pltpu.VMEM((2 * band, LANES), jnp.int32),
            pltpu.SMEM((band, 2 * LANES), jnp.int32),
            pltpu.VMEM((M // LANES, LANES), jnp.int32),
            pltpu.VMEM(coef.shape, f32),
            pltpu.VMEM(twiddle.shape, f32),
            pltpu.VMEM(inner.shape, bf16),
            pltpu.VMEM(outer.shape, bf16),
            pltpu.VMEM((blocks, 8, BLK), f32),
            pltpu.VMEM((4 * band, LANES), f32),
            pltpu.VMEM((4 * band, LANES), f32),
            pltpu.VMEM((2 * band, LANES), f32),
            pltpu.VMEM((2 * band, LANES), f32),
            pltpu.VMEM((4 * M // LANES, LANES), f32),
            pltpu.VMEM((band, LANES), f32),
            pltpu.VMEM((band, LANES), f32),
            pltpu.VMEM((lev, 4, owned, LANES), f32),
            pltpu.VMEM((4, lev, owned, LANES), f32),
            pltpu.SemaphoreType.DMA((9,)),
            pltpu.SemaphoreType.DMA((4,)),
            pltpu.SemaphoreType.DMA((4,)),
        ],
        compiler_params=pltpu.CompilerParams(collective_id=0, has_side_effects=True, vmem_limit_bytes=60 * 2**20),
        name="modes",
    )(
        cycle_ids,
        winds.reshape(3 * blocks, BLK),
        remap_w.reshape(2 * band, LANES),
        remap_col.reshape(2 * band, LANES),
        block_pick,
        wave_ids.reshape(M // LANES, LANES),
        coef,
        twiddle,
        inner,
        outer,
    )
    width = 512
    shape = jax.ShapeDtypeStruct((2 * lev * owned, degrees), f32)
    divergence, vorticity = pl.pallas_call(
        functools.partial(legendre_kernel, owned),
        grid=(degrees // width,),
        out_shape=(shape, shape),
        in_specs=[
            smem,
            pl.BlockSpec((4 * lev * owned, 2 * cycles), lambda j: (0, 0)),
            pl.BlockSpec((owned, cycles, width), lambda j: (0, 0, j)),
            pl.BlockSpec((owned, cycles, width), lambda j: (0, 0, j)),
        ],
        out_specs=(
            pl.BlockSpec((2 * lev * owned, width), lambda j: (0, j)),
            pl.BlockSpec((2 * lev * owned, width), lambda j: (0, j)),
        ),
        compiler_params=pltpu.CompilerParams(vmem_limit_bytes=60 * 2**20),
        name="legendre",
    )(wave_ids, left, legendre_a, legendre_b)
    whole = (2, lev, owned, degrees)
    return divergence.reshape(whole), vorticity.reshape(whole)


def solution(mesh):
    placed = (
        P(None, "lev", "band"),
        P(None, "band", None),
        P(None, "band", None),
        P(),
        P("band"),
        P(),
        P(("band", "lev"), None, None),
        P(("band", "lev"), None, None),
    )
    return jax.shard_map(
        local,
        mesh=mesh,
        in_specs=placed,
        out_specs=(P(None, None, ("band", "lev"), None), P(None, None, ("band", "lev"), None)),
        check_vma=False,
    )
```

```python
import functools
import math

import jax
import jax.numpy as jnp
import numpy as np
from jax import lax
from jax.experimental import pallas as pl
from jax.experimental.pallas import tpu as pltpu
from jax.sharding import PartitionSpec as P

NSIDE = 1024
NPHI = 4096
M = 2048
BLK = 128
PER = 12
TAPS = 4
LANES = 128
WIDTH = 512

f32 = jnp.float32
bf16 = jnp.bfloat16


def split(table):
    table = np.asarray(table, np.float32)
    high = table.astype(jnp.bfloat16)
    low = (table - high.astype(np.float32)).astype(jnp.bfloat16)
    return high, low


@functools.cache
def tables(band):
    rho = np.arange(2 * band)
    n = (rho % 2) * band + rho // 2
    b = np.arange(NPHI // (2 * band))
    mu = np.arange(LANES)
    m1 = np.arange(M // LANES)
    turn = 2.0 * np.pi / NPHI
    coef, twiddle, outer_hi, outer_lo = [], [], [], []
    for half in (0, 1):
        delta = 1.0 - 0.5 * half
        azimuth = turn * (2 * band * b[None, :] + n[:, None] + delta)
        zero = np.zeros_like(azimuth)
        cos, sin = np.cos(azimuth), np.sin(azimuth)
        coef.append(np.stack([np.concatenate([-sin, cos, zero, zero], 1), np.concatenate([cos, sin, zero, zero], 1)]))
        phi = turn * mu[None, :] * (n[:, None] + delta)
        twiddle.append(np.stack([np.cos(phi), np.sin(phi)]))
        psi = turn * LANES * m1[:, None] * (n[None, :] + delta)
        full = np.concatenate(
            [np.concatenate([np.cos(psi), np.sin(psi)], 1), np.concatenate([-np.sin(psi), np.cos(psi)], 1)], 0
        )
        high, low = split(full)
        outer_hi.append(high)
        outer_lo.append(low)
    angle = 2.0 * np.pi / b.size * (b[:, None] * mu[None, :])
    inner = np.tile(np.concatenate([np.cos(angle), -np.sin(angle)], 1), (4, 1))
    inner_hi, inner_lo = split(inner)
    return (
        np.stack(coef).astype(np.float32),
        np.stack(twiddle).astype(np.float32),
        np.stack([inner_hi, inner_lo]),
        np.stack([np.stack(outer_hi), np.stack(outer_lo)]),
    )


def dot(a, b):
    return jnp.dot(a, b, preferred_element_type=f32)


def high_low(x):
    high = x.astype(bf16)
    return high, (x - high.astype(f32)).astype(bf16)


def take(x, index):
    return jnp.take_along_axis(x, index, axis=1, mode="promise_in_bounds")


def modes_kernel(
    band,
    lev,
    cycle_ref,
    winds_hbm,
    weight_hbm,
    column_hbm,
    pick_hbm,
    wave_hbm,
    coef_hbm,
    twiddle_hbm,
    inner_hbm,
    outer_hbm,
    a_hbm,
    b_hbm,
    out_ref,
    leg_a,
    leg_b,
    winds,
    weight,
    column,
    pick,
    wave,
    coef,
    twiddle,
    inner,
    outer,
    table,
    request_out,
    request_in,
    reply_out,
    reply_in,
    spectrum,
    rows_out,
    rows_in,
    turned,
    levels_in,
    local_sem,
    send_sem,
    recv_sem,
    legendre_sem,
):
    me = lax.axis_index("band")
    my_lev = lax.axis_index("lev")
    barrier = pltpu.get_barrier_semaphore()

    def greet(i, carry):
        other = lax.rem(me + i, band)
        pl.semaphore_signal(barrier, 1, device_id=(other, my_lev), device_id_type=pl.DeviceIdType.MESH)
        return carry

    lax.fori_loop(1, band, greet, 0)
    for i in range(1, lev):
        other = lax.rem(my_lev + i, lev)
        pl.semaphore_signal(barrier, 1, device_id=(me, other), device_id_type=pl.DeviceIdType.MESH)

    window = jnp.minimum(me * PER // LANES, PER * band // LANES - 2)
    pick_at = me * PER - window * LANES
    loads = [
        pltpu.make_async_copy(source, target, local_sem.at[i])
        for i, (source, target) in enumerate(
            (
                (column_hbm, column),
                (weight_hbm, weight),
                (winds_hbm, winds),
                (pick_hbm.at[:, pl.ds(pl.multiple_of(window * LANES, LANES), 2 * LANES)], pick),
                (coef_hbm, coef),
                (twiddle_hbm, twiddle),
                (inner_hbm, inner),
                (outer_hbm, outer),
                (wave_hbm, wave),
            )
        )
    ]
    for load in loads:
        load.start()

    def to_band(source, target, other, phase):
        return pltpu.make_async_remote_copy(
            src_ref=source,
            dst_ref=target,
            send_sem=send_sem.at[phase],
            recv_sem=recv_sem.at[phase],
            device_id=(other, my_lev),
            device_id_type=pl.DeviceIdType.MESH,
        )

    loads[0].wait()
    loads[1].wait()
    turned_column = column[...].astype(f32).T
    turned_weight = weight[...].T
    for h in range(2):
        request_out[pl.ds(h, band, stride=4), :] = turned_column[h * band : (h + 1) * band]
        request_out[pl.ds(2 + h, band, stride=4), :] = turned_weight[h * band : (h + 1) * band]
    loads[2].wait()
    blocks = winds.shape[0] // 3
    for a in range(3):
        part = winds[pl.ds(a * blocks, blocks), :]
        table[:, a, :] = part
        table[:, 4 + a, :] = part
    pl.semaphore_wait(barrier, band - 1 + lev - 1)
    mine = pltpu.make_async_copy(
        request_out.at[pl.ds(4 * me, 4)], request_in.at[pl.ds(4 * me, 4)], recv_sem.at[0]
    )
    mine.start()

    def send_request(i, carry):
        other = lax.rem(me + i, band)
        to_band(request_out.at[pl.ds(4 * other, 4)], request_in.at[pl.ds(4 * me, 4)], other, 0).start()
        return carry

    lax.fori_loop(1, band, send_request, 0)
    legendre_loads = [
        pltpu.make_async_copy(a_hbm, leg_a, legendre_sem.at[0]),
        pltpu.make_async_copy(b_hbm, leg_b, legendre_sem.at[1]),
    ]
    for load in legendre_loads:
        load.start()
    loads[3].wait()
    pltpu.make_async_copy(request_in, request_in, recv_sem.at[0]).wait()

    sub = lax.broadcasted_iota(jnp.int32, (8, LANES), 0)
    lane = lax.broadcasted_iota(jnp.int32, (8, LANES), 1)
    upper = sub < 4
    own_group = (lane >> 5) == (sub & 3)

    def weigh(other):
        rows = [jnp.broadcast_to(request_in[pl.ds(4 * other + k, 1), :], (8, LANES)) for k in range(4)]
        where = jnp.where(upper, rows[0], rows[1]).astype(jnp.int32)
        scale = jnp.where(upper, rows[2], rows[3])
        within, block = where & (BLK - 1), where >> 7
        total = jnp.zeros((8, LANES), f32)
        for c in range(PER):
            piece = table[pick[other, pick_at + c]]
            total = jnp.where(block == c, take(piece, within), total)
        total = total * scale
        total = total + pltpu.roll(total, 64, 1)
        total = total + pltpu.roll(total, 32, 1)
        total = jnp.where(own_group, total, 0.0)
        total = total + pltpu.roll(total, 1, 0)
        total = total + pltpu.roll(total, 2, 0)
        reply_out[pl.ds(2 * other, 1), :] = total[3:4]
        reply_out[pl.ds(2 * other + 1, 1), :] = total[7:8]

    weigh(me)
    mine = pltpu.make_async_copy(
        reply_out.at[pl.ds(2 * me, 2)], reply_in.at[pl.ds(2 * me, 2)], recv_sem.at[1]
    )
    mine.start()
    group = 7

    def send_reply(i, carry):
        for u in range(group):
            weigh(lax.rem(me + 1 + i * group + u, band))
        for u in range(group):
            other = lax.rem(me + 1 + i * group + u, band)
            to_band(reply_out.at[pl.ds(2 * other, 2)], reply_in.at[pl.ds(2 * me, 2)], other, 1).start()
        return carry

    lax.fori_loop(0, (band - 1) // group, send_reply, 0)
    for load in loads[4:]:
        load.wait()
    pltpu.make_async_copy(reply_in, reply_in, recv_sem.at[1]).wait()

    number = cycle_ref[0]
    odd = (jnp.full((2 * band, LANES), number, jnp.int32) & 1) == 1
    odd_thin = (jnp.full((2 * M // LANES, 4 * band), number, jnp.int32) & 1) == 1

    def by_parity(table, *at):
        return jnp.where(odd, table[(0, *at)], table[(1, *at)])

    cos_theta = 4.0 / 3.0 - 2.0 * jnp.full((2 * band, LANES), number, jnp.int32).astype(f32) / (3.0 * NSIDE)
    sin_theta = jnp.sqrt(1.0 - cos_theta * cos_theta)
    component = lax.broadcasted_iota(jnp.int32, (2 * band, LANES), 1) >> 5
    samples = reply_in[...]
    east = samples * by_parity(coef, 0)
    north = samples * jnp.where(component == 2, sin_theta, -cos_theta * by_parity(coef, 1))
    high, low = high_low(jnp.concatenate([east, north], 0))
    section = dot(high, inner[0]) + dot(low, inner[0]) + dot(high, inner[1])
    cos, sin = by_parity(twiddle, 0), by_parity(twiddle, 1)
    cos, sin = jnp.concatenate([cos, cos], 0), jnp.concatenate([sin, sin], 0)
    real, imag = section[:, :LANES], section[:, LANES:]
    real, imag = real * cos + imag * sin, imag * cos - real * sin
    n = 2 * band
    high, low = high_low(
        jnp.concatenate(
            [jnp.concatenate([real[:n], real[n:]], 1), jnp.concatenate([imag[:n], imag[n:]], 1)], 0
        )
    )
    outer_hi = jnp.where(odd_thin, outer[0, 0], outer[0, 1])
    outer_lo = jnp.where(odd_thin, outer[1, 0], outer[1, 1])
    full = dot(outer_hi, high) + dot(outer_hi, low) + dot(outer_lo, high)
    full = full.astype(bf16).astype(f32)
    rows = M // LANES
    for f, (r, c) in enumerate(((0, 0), (1, 0), (0, 1), (1, 1))):
        spectrum[pl.ds(f * rows, rows), :] = full[r * rows : (r + 1) * rows, c * LANES : (c + 1) * LANES]

    wave_row, wave_lane = wave[...] >> 7, wave[...] & (LANES - 1)
    field = (lane >> 3) & 3
    spot = (lane >> 5) * 8 + (lane & 7)
    for h in range(rows // 8):
        row_of, lane_of = wave_row[8 * h : 8 * h + 8], wave_lane[8 * h : 8 * h + 8]
        ordered = []
        for f in range(4):
            picked = jnp.zeros((8, LANES), f32)
            for r in range(rows):
                source = jnp.broadcast_to(spectrum[pl.ds(f * rows + r, 1), :], (8, LANES))
                picked = jnp.where(row_of == r, take(source, lane_of), picked)
            ordered.append(picked)
        for b in range(4):
            packed = jnp.zeros((8, LANES), f32)
            for f in range(4):
                packed = jnp.where(field == f, take(ordered[f], spot + 32 * b), packed)
            rows_out[pl.ds(b * rows + 8 * h, 8), :] = packed

    def row_for(other):
        return lax.rem(other, 4) * rows + other // 4

    mine = pltpu.make_async_copy(rows_out.at[pl.ds(row_for(me), 1)], rows_in.at[pl.ds(me, 1)], recv_sem.at[2])
    mine.start()

    def send_rows(i, carry):
        other = lax.rem(me + i, band)
        to_band(rows_out.at[pl.ds(row_for(other), 1)], rows_in.at[pl.ds(me, 1)], other, 2).start()
        return carry

    lax.fori_loop(1, band, send_rows, 0)
    pltpu.make_async_copy(rows_in, rows_in, recv_sem.at[2]).wait()

    arrived = rows_in[...]
    turned[...] = jnp.concatenate([arrived, arrived], 0).T.reshape(turned.shape)
    mine = pltpu.make_async_copy(turned.at[my_lev], levels_in.at[:, my_lev], recv_sem.at[3])
    mine.start()

    def to_level(other):
        return pltpu.make_async_remote_copy(
            src_ref=turned.at[other],
            dst_ref=levels_in.at[:, my_lev],
            send_sem=send_sem.at[3],
            recv_sem=recv_sem.at[3],
            device_id=(me, other),
            device_id_type=pl.DeviceIdType.MESH,
        )

    for i in range(1, lev):
        to_level(lax.rem(my_lev + i, lev)).start()
    pltpu.make_async_copy(levels_in, levels_in, recv_sem.at[3]).wait()

    first = lax.broadcasted_iota(jnp.int32, (8, LANES), 1) < band
    sign_a, sign_b = (-1.0, 1.0, -1.0, 1.0), (-1.0, -1.0, 1.0, 1.0)
    for o in range(4):
        for v in range(lev):
            out_ref[pl.ds((o * lev + v) * 8, 8), :] = jnp.where(
                first, sign_a[o] * levels_in[o ^ 1, v], sign_b[o] * levels_in[o ^ 2, v]
            )

    for load in legendre_loads:
        load.wait()
    pltpu.make_async_copy(request_out.at[pl.ds(0, 4 * (band - 1))], request_out.at[pl.ds(0, 4 * (band - 1))], send_sem.at[0]).wait()
    pltpu.make_async_copy(reply_out.at[pl.ds(0, 2 * (band - 1))], reply_out.at[pl.ds(0, 2 * (band - 1))], send_sem.at[1]).wait()
    pltpu.make_async_copy(rows_out.at[pl.ds(0, band - 1)], rows_out.at[pl.ds(0, band - 1)], send_sem.at[2]).wait()
    pltpu.make_async_copy(turned.at[pl.ds(0, lev - 1)], turned.at[pl.ds(0, lev - 1)], send_sem.at[3]).wait()


def legendre_kernel(wave_ref, left_ref, a_ref, b_ref, div_hbm, vort_hbm, div, vort, store_sem):
    me = lax.axis_index("band") * lax.axis_size("lev") + lax.axis_index("lev")
    owned, _, degrees = a_ref.shape
    half = left_ref.shape[0] // 2
    left = left_ref[...]
    slot = lax.broadcasted_iota(jnp.int32, left.shape, 0) % owned
    pieces = [jnp.where(slot == i, left, 0.0).astype(bf16) for i in range(owned)]
    pieces = [jnp.concatenate(pieces[i : i + 2], 1) for i in range(0, owned, 2)]
    row = lax.broadcasted_iota(jnp.int32, (owned, WIDTH), 0)
    lowest = jnp.zeros((owned, WIDTH), jnp.int32)
    for i in range(owned):
        lowest = jnp.where(row == i, wave_ref[me * owned + i], lowest)
    stores = []
    for j in range(degrees // WIDTH):
        at = pl.ds(j * WIDTH, WIDTH)
        total = jnp.zeros((2 * half, WIDTH), f32)
        for i in range(0, owned, 2):
            right = jnp.concatenate([a_ref[i, :, at], b_ref[i, :, at], a_ref[i + 1, :, at], b_ref[i + 1, :, at]], 0)
            total = total + dot(pieces[i // 2], right)
        keep = j * WIDTH + lax.broadcasted_iota(jnp.int32, (owned, WIDTH), 1) >= lowest
        for r in range(0, half, owned):
            div[r : r + owned, at] = jnp.where(keep, total[r : r + owned], 0.0)
            vort[r : r + owned, at] = jnp.where(keep, total[half + r : half + r + owned], 0.0)
        for k, (source, target) in enumerate(((div, div_hbm), (vort, vort_hbm))):
            stores.append(pltpu.make_async_copy(source.at[:, at], target.at[:, at], store_sem.at[2 * j + k]))
            stores[-1].start()
    for store in stores:
        store.wait()


def local(winds, remap_w, remap_col, block_pick, cycle_ids, wave_ids, legendre_a, legendre_b):
    band, lev = lax.axis_size("band"), lax.axis_size("lev")
    coef, twiddle, inner, outer = tables(band)
    columns = winds.shape[2]
    owned, cycles, degrees = legendre_a.shape
    blocks = columns // BLK
    hbm = pl.BlockSpec(memory_space=pltpu.HBM)
    smem = pl.BlockSpec(memory_space=pltpu.SMEM)
    vmem = pl.BlockSpec(memory_space=pltpu.VMEM)
    left, leg_a, leg_b = pl.pallas_call(
        functools.partial(modes_kernel, band, lev),
        out_shape=(
            pltpu.VMEM((4 * lev * owned, 2 * cycles), f32),
            pltpu.VMEM(legendre_a.shape, bf16),
            pltpu.VMEM(legendre_b.shape, bf16),
        ),
        in_specs=[smem] + [hbm] * 11,
        out_specs=(vmem, vmem, vmem),
        scratch_shapes=[
            pltpu.VMEM((3 * blocks, BLK), f32),
            pltpu.VMEM((2 * band, LANES), f32),
            pltpu.VMEM((2 * band, LANES), jnp.int32),
            pltpu.SMEM((band, 2 * LANES), jnp.int32),
            pltpu.VMEM((M // LANES, LANES), jnp.int32),
            pltpu.VMEM(coef.shape, f32),
            pltpu.VMEM(twiddle.shape, f32),
            pltpu.VMEM(inner.shape, bf16),
            pltpu.VMEM(outer.shape, bf16),
            pltpu.VMEM((blocks, 8, BLK), f32),
            pltpu.VMEM((4 * band, LANES), f32),
            pltpu.VMEM((4 * band, LANES), f32),
            pltpu.VMEM((2 * band, LANES), f32),
            pltpu.VMEM((2 * band, LANES), f32),
            pltpu.VMEM((4 * M // LANES, LANES), f32),
            pltpu.VMEM((band, LANES), f32),
            pltpu.VMEM((band, LANES), f32),
            pltpu.VMEM((lev, 4, owned, LANES), f32),
            pltpu.VMEM((4, lev, owned, LANES), f32),
            pltpu.SemaphoreType.DMA((9,)),
            pltpu.SemaphoreType.DMA((4,)),
            pltpu.SemaphoreType.DMA((4,)),
            pltpu.SemaphoreType.DMA((2,)),
        ],
        compiler_params=pltpu.CompilerParams(collective_id=0, has_side_effects=True, vmem_limit_bytes=52 * 2**20),
        name="modes",
    )(
        cycle_ids,
        winds.reshape(3 * blocks, BLK),
        remap_w.reshape(2 * band, LANES),
        remap_col.reshape(2 * band, LANES),
        block_pick,
        wave_ids.reshape(M // LANES, LANES),
        coef,
        twiddle,
        inner,
        outer,
        legendre_a,
        legendre_b,
    )
    shape = jax.ShapeDtypeStruct((2 * lev * owned, degrees), f32)
    divergence, vorticity = pl.pallas_call(
        legendre_kernel,
        out_shape=(shape, shape),
        in_specs=[smem, vmem, vmem, vmem],
        out_specs=(hbm, hbm),
        scratch_shapes=[
            pltpu.VMEM(shape.shape, f32),
            pltpu.VMEM(shape.shape, f32),
            pltpu.SemaphoreType.DMA((2 * degrees // WIDTH,)),
        ],
        compiler_params=pltpu.CompilerParams(vmem_limit_bytes=32 * 2**20),
        name="legendre",
    )(wave_ids, left, leg_a, leg_b)
    whole = (2, lev, owned, degrees)
    return divergence.reshape(whole), vorticity.reshape(whole)


def solution(mesh):
    placed = (
        P(None, "lev", "band"),
        P(None, "band", None),
        P(None, "band", None),
        P(),
        P("band"),
        P(),
        P(("band", "lev"), None, None),
        P(("band", "lev"), None, None),
    )
    return jax.shard_map(
        local,
        mesh=mesh,
        in_specs=placed,
        out_specs=(P(None, None, ("band", "lev"), None), P(None, None, ("band", "lev"), None)),
        check_vma=False,
    )
```

```python
import functools
import math

import jax
import jax.numpy as jnp
import numpy as np
from jax import lax
from jax.experimental import pallas as pl
from jax.experimental.pallas import tpu as pltpu
from jax.sharding import PartitionSpec as P

NSIDE = 1024
NPHI = 4096
M = 2048
BLK = 128
PER = 12
TAPS = 4
LANES = 128
GROUP = 8
WIDTH = 512

f32 = jnp.float32
bf16 = jnp.bfloat16


def split(table):
    table = np.asarray(table, np.float32)
    high = table.astype(jnp.bfloat16)
    low = (table - high.astype(np.float32)).astype(jnp.bfloat16)
    return high, low


@functools.cache
def tables(band):
    rho = np.arange(2 * band)
    n = (rho % 2) * band + rho // 2
    b = np.arange(NPHI // (2 * band))
    mu = np.arange(LANES)
    m1 = np.arange(M // LANES)
    turn = 2.0 * np.pi / NPHI
    coef, twiddle, outer_hi, outer_lo = [], [], [], []
    for half in (0, 1):
        delta = 1.0 - 0.5 * half
        azimuth = turn * (2 * band * b[None, :] + n[:, None] + delta)
        zero = np.zeros_like(azimuth)
        cos, sin = np.cos(azimuth), np.sin(azimuth)
        coef.append(np.stack([np.concatenate([-sin, cos, zero, zero], 1), np.concatenate([cos, sin, zero, zero], 1)]))
        phi = turn * mu[None, :] * (n[:, None] + delta)
        twiddle.append(np.stack([np.cos(phi), np.sin(phi)]))
        psi = turn * LANES * m1[:, None] * (n[None, :] + delta)
        full = np.concatenate(
            [np.concatenate([np.cos(psi), np.sin(psi)], 1), np.concatenate([-np.sin(psi), np.cos(psi)], 1)], 0
        )
        high, low = split(full)
        outer_hi.append(high)
        outer_lo.append(low)
    angle = 2.0 * np.pi / b.size * (b[:, None] * mu[None, :])
    inner = np.tile(np.concatenate([np.cos(angle), -np.sin(angle)], 1), (4, 1))
    inner_hi, inner_lo = split(inner)
    return (
        np.stack(coef).astype(np.float32),
        np.stack(twiddle).astype(np.float32),
        np.stack([inner_hi, inner_lo]),
        np.stack([np.stack(outer_hi), np.stack(outer_lo)]),
    )


def dot(a, b):
    return jnp.dot(a, b, preferred_element_type=f32)


def far_first(i, count):
    return count // 2 + (1 - 2 * (i % 2)) * ((i + 1) // 2)


def high_low(x):
    high = x.astype(bf16)
    return high, (x - high.astype(f32)).astype(bf16)


def take(x, index):
    return jnp.take_along_axis(x, index, axis=1, mode="promise_in_bounds")


def modes_kernel(
    band,
    lev,
    cycle_ref,
    winds_hbm,
    weight_hbm,
    column_hbm,
    pick_hbm,
    wave_hbm,
    coef_hbm,
    twiddle_hbm,
    inner_hbm,
    outer_hbm,
    a_hbm,
    b_hbm,
    out_ref,
    leg_a,
    leg_b,
    winds,
    weight,
    column,
    pick,
    wave,
    coef,
    twiddle,
    inner,
    outer,
    table,
    request_out,
    request_in,
    reply_out,
    reply_in,
    spectrum,
    rows_out,
    rows_in,
    local_sem,
    send_sem,
    recv_sem,
    legendre_sem,
):
    me = lax.axis_index("band")
    my_lev = lax.axis_index("lev")
    barrier = pltpu.get_barrier_semaphore()

    plane, place = lax.div(me, GROUP), lax.rem(me, GROUP)
    planes = band // GROUP
    places = [lax.rem(place + far_first(k, GROUP), GROUP) for k in range(GROUP)]
    my_levels = [lax.rem(my_lev + far_first(k, lev), lev) for k in range(lev)]

    def each_plane(act):
        def step(k, carry):
            odd = lax.rem(k, 2)
            ahead = planes // 2 + (1 - 2 * odd) * lax.div(k + 1, 2)
            base = lax.rem(plane + ahead, planes) * GROUP
            act([base + p for p in places])
            return carry

        lax.fori_loop(0, planes - 1, step, 0)
        act([plane * GROUP + p for p in places[:-1]])

    def greet(others):
        for other in others:
            pl.semaphore_signal(barrier, 1, device_id=(other, my_lev), device_id_type=pl.DeviceIdType.MESH)

    each_plane(greet)
    for i in range(1, lev):
        other = lax.rem(my_lev + i, lev)
        pl.semaphore_signal(barrier, 1, device_id=(me, other), device_id_type=pl.DeviceIdType.MESH)

    window = jnp.minimum(me * PER // LANES, PER * band // LANES - 2)
    pick_at = me * PER - window * LANES
    loads = [
        pltpu.make_async_copy(source, target, local_sem.at[i])
        for i, (source, target) in enumerate(
            (
                (column_hbm, column),
                (weight_hbm, weight),
                (winds_hbm, winds),
                (pick_hbm.at[:, pl.ds(pl.multiple_of(window * LANES, LANES), 2 * LANES)], pick),
                (coef_hbm, coef),
                (twiddle_hbm, twiddle),
                (inner_hbm, inner),
                (outer_hbm, outer),
                (wave_hbm, wave),
            )
        )
    ]
    for load in loads:
        load.start()

    def to_band(source, target, other, phase):
        return pltpu.make_async_remote_copy(
            src_ref=source,
            dst_ref=target,
            send_sem=send_sem.at[phase],
            recv_sem=recv_sem.at[phase],
            device_id=(other, my_lev),
            device_id_type=pl.DeviceIdType.MESH,
        )

    loads[0].wait()
    loads[1].wait()
    turned_column = column[...].astype(f32).T
    turned_weight = weight[...].T
    for h in range(2):
        request_out[pl.ds(h, band, stride=4), :] = turned_column[h * band : (h + 1) * band]
        request_out[pl.ds(2 + h, band, stride=4), :] = turned_weight[h * band : (h + 1) * band]
    loads[2].wait()
    blocks = winds.shape[0] // 3
    for a in range(3):
        part = winds[pl.ds(a * blocks, blocks), :]
        table[:, a, :] = part
        table[:, 4 + a, :] = part
    pl.semaphore_wait(barrier, band - 1 + lev - 1)
    mine = pltpu.make_async_copy(
        request_out.at[pl.ds(4 * me, 4)], request_in.at[pl.ds(4 * me, 4)], recv_sem.at[0]
    )
    mine.start()

    def send_request(others):
        for other in others:
            to_band(request_out.at[pl.ds(4 * other, 4)], request_in.at[pl.ds(4 * me, 4)], other, 0).start()

    each_plane(send_request)
    legendre_loads = [
        pltpu.make_async_copy(a_hbm, leg_a, legendre_sem.at[0]),
        pltpu.make_async_copy(b_hbm, leg_b, legendre_sem.at[1]),
    ]
    for load in legendre_loads:
        load.start()
    loads[3].wait()
    pltpu.make_async_copy(request_in, request_in, recv_sem.at[0]).wait()

    sub = lax.broadcasted_iota(jnp.int32, (8, LANES), 0)
    lane = lax.broadcasted_iota(jnp.int32, (8, LANES), 1)
    upper = sub < 4
    own_group = (lane >> 5) == (sub & 3)

    def weigh(other):
        rows = [jnp.broadcast_to(request_in[pl.ds(4 * other + k, 1), :], (8, LANES)) for k in range(4)]
        where = jnp.where(upper, rows[0], rows[1]).astype(jnp.int32)
        scale = jnp.where(upper, rows[2], rows[3])
        within, block = where & (BLK - 1), where >> 7
        total = jnp.zeros((8, LANES), f32)
        for c in range(PER):
            piece = table[pick[other, pick_at + c]]
            total = jnp.where(block == c, take(piece, within), total)
        total = total * scale
        total = total + pltpu.roll(total, 64, 1)
        total = total + pltpu.roll(total, 32, 1)
        total = jnp.where(own_group, total, 0.0)
        total = total + pltpu.roll(total, 1, 0)
        total = total + pltpu.roll(total, 2, 0)
        reply_out[pl.ds(2 * other, 1), :] = total[3:4]
        reply_out[pl.ds(2 * other + 1, 1), :] = total[7:8]

    def send_reply(others):
        for other in others:
            weigh(other)
        for other in others:
            to_band(reply_out.at[pl.ds(2 * other, 2)], reply_in.at[pl.ds(2 * me, 2)], other, 1).start()

    each_plane(send_reply)
    weigh(me)
    mine = pltpu.make_async_copy(
        reply_out.at[pl.ds(2 * me, 2)], reply_in.at[pl.ds(2 * me, 2)], recv_sem.at[1]
    )
    mine.start()
    for load in loads[4:]:
        load.wait()
    pltpu.make_async_copy(reply_in, reply_in, recv_sem.at[1]).wait()

    number = cycle_ref[0]
    odd = (jnp.full((2 * band, LANES), number, jnp.int32) & 1) == 1
    odd_thin = (jnp.full((2 * M // LANES, 4 * band), number, jnp.int32) & 1) == 1

    def by_parity(table, *at):
        return jnp.where(odd, table[(0, *at)], table[(1, *at)])

    cos_theta = 4.0 / 3.0 - 2.0 * jnp.full((2 * band, LANES), number, jnp.int32).astype(f32) / (3.0 * NSIDE)
    sin_theta = jnp.sqrt(1.0 - cos_theta * cos_theta)
    component = lax.broadcasted_iota(jnp.int32, (2 * band, LANES), 1) >> 5
    samples = reply_in[...]
    east = samples * by_parity(coef, 0)
    north = samples * jnp.where(component == 2, sin_theta, -cos_theta * by_parity(coef, 1))
    high, low = high_low(jnp.concatenate([east, north], 0))
    section = dot(high, inner[0]) + dot(low, inner[0]) + dot(high, inner[1])
    cos, sin = by_parity(twiddle, 0), by_parity(twiddle, 1)
    cos, sin = jnp.concatenate([cos, cos], 0), jnp.concatenate([sin, sin], 0)
    real, imag = section[:, :LANES], section[:, LANES:]
    real, imag = real * cos + imag * sin, imag * cos - real * sin
    n = 2 * band
    high, low = high_low(
        jnp.concatenate(
            [jnp.concatenate([real[:n], real[n:]], 1), jnp.concatenate([imag[:n], imag[n:]], 1)], 0
        )
    )
    outer_hi = jnp.where(odd_thin, outer[0, 0], outer[0, 1])
    outer_lo = jnp.where(odd_thin, outer[1, 0], outer[1, 1])
    full = dot(outer_hi, high) + dot(outer_hi, low) + dot(outer_lo, high)
    full = full.astype(bf16).astype(f32)
    rows = M // LANES
    for f, (r, c) in enumerate(((0, 0), (1, 0), (0, 1), (1, 1))):
        spectrum[pl.ds(f * rows, rows), :] = full[r * rows : (r + 1) * rows, c * LANES : (c + 1) * LANES]

    wave_row, wave_lane = wave[...] >> 7, wave[...] & (LANES - 1)
    field = (lane >> 3) & 3
    spot = (lane >> 5) * 8 + (lane & 7)
    for h in range(rows // 8):
        row_of, lane_of = wave_row[8 * h : 8 * h + 8], wave_lane[8 * h : 8 * h + 8]
        ordered = []
        for f in range(4):
            picked = jnp.zeros((8, LANES), f32)
            for r in range(rows):
                source = jnp.broadcast_to(spectrum[pl.ds(f * rows + r, 1), :], (8, LANES))
                picked = jnp.where(row_of == r, take(source, lane_of), picked)
            ordered.append(picked)
        for b in range(4):
            packed = jnp.zeros((8, LANES), f32)
            for f in range(4):
                packed = jnp.where(field == f, take(ordered[f], spot + 32 * b), packed)
            rows_out[pl.ds(b * rows + 8 * h, 8), :] = packed

    def row_for(other):
        return lax.rem(other, 4) * rows + lax.div(other, 4)

    def send_row(other, levels):
        for v in levels:
            pltpu.make_async_remote_copy(
                src_ref=rows_out.at[pl.ds(row_for(other), 1)],
                dst_ref=rows_in.at[pl.ds(my_lev * band + me, 1)],
                send_sem=send_sem.at[2],
                recv_sem=recv_sem.at[2],
                device_id=(other, v),
                device_id_type=pl.DeviceIdType.MESH,
            ).start()

    def send_rows(others):
        for other in others:
            send_row(other, my_levels)

    each_plane(send_rows)
    send_row(me, my_levels[:-1])
    mine = pltpu.make_async_copy(
        rows_out.at[pl.ds(row_for(me), 1)], rows_in.at[pl.ds(my_lev * band + me, 1)], recv_sem.at[2]
    )
    mine.start()
    pltpu.make_async_copy(rows_in, rows_in, recv_sem.at[2]).wait()

    level = lax.broadcasted_iota(jnp.int32, (band, LANES), 1) >> 5
    merged = jnp.zeros((band, LANES), f32)
    for v in range(lev):
        shifted = pltpu.roll(rows_in[pl.ds(v * band, band), :], lax.rem(v - my_lev + lev, lev) * 32, 1)
        merged = jnp.where(level == v, shifted, merged)
    turned = jnp.concatenate([merged, merged], 0).T
    first = lane < band
    sign_a, sign_b = (-1.0, 1.0, -1.0, 1.0), (-1.0, -1.0, 1.0, 1.0)

    def piece_of(v, f):
        return turned[(v * 4 + f) * 8 : (v * 4 + f) * 8 + 8]

    for o in range(4):
        for v in range(lev):
            out_ref[pl.ds((o * lev + v) * 8, 8), :] = jnp.where(
                first, sign_a[o] * piece_of(v, o ^ 1), sign_b[o] * piece_of(v, o ^ 2)
            )
    for load in legendre_loads:
        load.wait()
    pltpu.make_async_copy(request_out.at[pl.ds(0, 4 * (band - 1))], request_out.at[pl.ds(0, 4 * (band - 1))], send_sem.at[0]).wait()
    pltpu.make_async_copy(reply_out.at[pl.ds(0, 2 * (band - 1))], reply_out.at[pl.ds(0, 2 * (band - 1))], send_sem.at[1]).wait()
    sent = rows_in.at[pl.ds(0, lev * band - 1)]
    pltpu.make_async_copy(sent, sent, send_sem.at[2]).wait()


def legendre_kernel(wave_ref, left_ref, a_ref, b_ref, div_hbm, vort_hbm, div, vort, store_sem):
    me = lax.axis_index("band") * lax.axis_size("lev") + lax.axis_index("lev")
    owned, _, degrees = a_ref.shape
    half = left_ref.shape[0] // 2
    left = left_ref[...]
    slot = lax.broadcasted_iota(jnp.int32, left.shape, 0) % owned
    pieces = [jnp.where(slot == i, left, 0.0).astype(bf16) for i in range(owned)]
    pieces = [jnp.concatenate(pieces[i : i + 2], 1) for i in range(0, owned, 2)]
    row = lax.broadcasted_iota(jnp.int32, (owned, WIDTH), 0)
    lowest = jnp.zeros((owned, WIDTH), jnp.int32)
    for i in range(owned):
        lowest = jnp.where(row == i, wave_ref[me * owned + i], lowest)
    stores = []
    for j in range(degrees // WIDTH):
        at = pl.ds(j * WIDTH, WIDTH)
        total = jnp.zeros((2 * half, WIDTH), f32)
        for i in range(0, owned, 2):
            right = jnp.concatenate([a_ref[i, :, at], b_ref[i, :, at], a_ref[i + 1, :, at], b_ref[i + 1, :, at]], 0)
            total = total + dot(pieces[i // 2], right)
        keep = j * WIDTH + lax.broadcasted_iota(jnp.int32, (owned, WIDTH), 1) >= lowest
        for r in range(0, half, owned):
            div[r : r + owned, at] = jnp.where(keep, total[r : r + owned], 0.0)
            vort[r : r + owned, at] = jnp.where(keep, total[half + r : half + r + owned], 0.0)
        for k, (source, target) in enumerate(((div, div_hbm), (vort, vort_hbm))):
            stores.append(pltpu.make_async_copy(source.at[:, at], target.at[:, at], store_sem.at[2 * j + k]))
            stores[-1].start()
    for store in stores:
        store.wait()


def local(winds, remap_w, remap_col, block_pick, cycle_ids, wave_ids, legendre_a, legendre_b):
    band, lev = lax.axis_size("band"), lax.axis_size("lev")
    coef, twiddle, inner, outer = tables(band)
    columns = winds.shape[2]
    owned, cycles, degrees = legendre_a.shape
    blocks = columns // BLK
    hbm = pl.BlockSpec(memory_space=pltpu.HBM)
    smem = pl.BlockSpec(memory_space=pltpu.SMEM)
    vmem = pl.BlockSpec(memory_space=pltpu.VMEM)
    left, leg_a, leg_b = pl.pallas_call(
        functools.partial(modes_kernel, band, lev),
        out_shape=(
            pltpu.VMEM((4 * lev * owned, 2 * cycles), f32),
            pltpu.VMEM(legendre_a.shape, bf16),
            pltpu.VMEM(legendre_b.shape, bf16),
        ),
        in_specs=[smem] + [hbm] * 11,
        out_specs=(vmem, vmem, vmem),
        scratch_shapes=[
            pltpu.VMEM((3 * blocks, BLK), f32),
            pltpu.VMEM((2 * band, LANES), f32),
            pltpu.VMEM((2 * band, LANES), jnp.int32),
            pltpu.SMEM((band, 2 * LANES), jnp.int32),
            pltpu.VMEM((M // LANES, LANES), jnp.int32),
            pltpu.VMEM(coef.shape, f32),
            pltpu.VMEM(twiddle.shape, f32),
            pltpu.VMEM(inner.shape, bf16),
            pltpu.VMEM(outer.shape, bf16),
            pltpu.VMEM((blocks, 8, BLK), f32),
            pltpu.VMEM((4 * band, LANES), f32),
            pltpu.VMEM((4 * band, LANES), f32),
            pltpu.VMEM((2 * band, LANES), f32),
            pltpu.VMEM((2 * band, LANES), f32),
            pltpu.VMEM((4 * M // LANES, LANES), f32),
            pltpu.VMEM((band, LANES), f32),
            pltpu.VMEM((lev * band, LANES), f32),
            pltpu.SemaphoreType.DMA((9,)),
            pltpu.SemaphoreType.DMA((3,)),
            pltpu.SemaphoreType.DMA((3,)),
            pltpu.SemaphoreType.DMA((2,)),
        ],
        compiler_params=pltpu.CompilerParams(collective_id=0, has_side_effects=True, vmem_limit_bytes=52 * 2**20),
        name="modes",
    )(
        cycle_ids,
        winds.reshape(3 * blocks, BLK),
        remap_w.reshape(2 * band, LANES),
        remap_col.reshape(2 * band, LANES),
        block_pick,
        wave_ids.reshape(M // LANES, LANES),
        coef,
        twiddle,
        inner,
        outer,
        legendre_a,
        legendre_b,
    )
    shape = jax.ShapeDtypeStruct((2 * lev * owned, degrees), f32)
    divergence, vorticity = pl.pallas_call(
        legendre_kernel,
        out_shape=(shape, shape),
        in_specs=[smem, vmem, vmem, vmem],
        out_specs=(hbm, hbm),
        scratch_shapes=[
            pltpu.VMEM(shape.shape, f32),
            pltpu.VMEM(shape.shape, f32),
            pltpu.SemaphoreType.DMA((2 * degrees // WIDTH,)),
        ],
        compiler_params=pltpu.CompilerParams(vmem_limit_bytes=32 * 2**20),
        name="legendre",
    )(wave_ids, left, leg_a, leg_b)
    whole = (2, lev, owned, degrees)
    return divergence.reshape(whole), vorticity.reshape(whole)


def solution(mesh):
    placed = (
        P(None, "lev", "band"),
        P(None, "band", None),
        P(None, "band", None),
        P(),
        P("band"),
        P(),
        P(("band", "lev"), None, None),
        P(("band", "lev"), None, None),
    )
    return jax.shard_map(
        local,
        mesh=mesh,
        in_specs=placed,
        out_specs=(P(None, None, ("band", "lev"), None), P(None, None, ("band", "lev"), None)),
        check_vma=False,
    )
```

```python
import functools
import math

import jax
import jax.numpy as jnp
import numpy as np
from jax import lax
from jax.experimental import pallas as pl
from jax.experimental.pallas import tpu as pltpu
from jax.sharding import PartitionSpec as P

NSIDE = 1024
NPHI = 4096
M = 2048
BLK = 128
PER = 12
TAPS = 4
LANES = 128
GROUP = 8
WIDTH = 512

f32 = jnp.float32
bf16 = jnp.bfloat16


def split(table):
    table = np.asarray(table, np.float32)
    high = table.astype(jnp.bfloat16)
    low = (table - high.astype(np.float32)).astype(jnp.bfloat16)
    return high, low


@functools.cache
def tables(band):
    rho = np.arange(2 * band)
    n = (rho % 2) * band + rho // 2
    b = np.arange(NPHI // (2 * band))
    mu = np.arange(LANES)
    m1 = np.arange(M // LANES)
    turn = 2.0 * np.pi / NPHI
    coef, twiddle, outer_hi, outer_lo = [], [], [], []
    for half in (0, 1):
        delta = 1.0 - 0.5 * half
        azimuth = turn * (2 * band * b[None, :] + n[:, None] + delta)
        zero = np.zeros_like(azimuth)
        cos, sin = np.cos(azimuth), np.sin(azimuth)
        coef.append(np.stack([np.concatenate([-sin, cos, zero, zero], 1), np.concatenate([cos, sin, zero, zero], 1)]))
        phi = turn * mu[None, :] * (n[:, None] + delta)
        twiddle.append(np.stack([np.cos(phi), np.sin(phi)]))
        psi = turn * LANES * m1[:, None] * (n[None, :] + delta)
        full = np.concatenate(
            [np.concatenate([np.cos(psi), np.sin(psi)], 1), np.concatenate([-np.sin(psi), np.cos(psi)], 1)], 0
        )
        high, low = split(full)
        outer_hi.append(high)
        outer_lo.append(low)
    angle = 2.0 * np.pi / b.size * (b[:, None] * mu[None, :])
    inner = np.tile(np.concatenate([np.cos(angle), -np.sin(angle)], 1), (4, 1))
    inner_hi, inner_lo = split(inner)
    return (
        np.stack(coef).astype(np.float32),
        np.stack(twiddle).astype(np.float32),
        np.stack([inner_hi, inner_lo]),
        np.stack([np.stack(outer_hi), np.stack(outer_lo)]),
    )


def dot(a, b):
    return jnp.dot(a, b, preferred_element_type=f32)


def far_first(i, count):
    return count // 2 + (1 - 2 * (i % 2)) * ((i + 1) // 2)


def high_low(x):
    high = x.astype(bf16)
    return high, (x - high.astype(f32)).astype(bf16)


def take(x, index):
    return jnp.take_along_axis(x, index, axis=1, mode="promise_in_bounds")


def modes_kernel(
    band,
    lev,
    cycle_ref,
    winds_hbm,
    weight_hbm,
    column_hbm,
    pick_hbm,
    wave_hbm,
    coef_hbm,
    twiddle_hbm,
    inner_hbm,
    outer_hbm,
    a_hbm,
    b_hbm,
    out_ref,
    leg_a,
    leg_b,
    winds,
    weight,
    column,
    pick,
    wave,
    coef,
    twiddle,
    inner,
    outer,
    table,
    request_out,
    request_in,
    taps,
    reply_out,
    reply_in,
    spectrum,
    rows_out,
    rows_in,
    local_sem,
    send_sem,
    recv_sem,
    legendre_sem,
):
    me = lax.axis_index("band")
    my_lev = lax.axis_index("lev")
    barrier = pltpu.get_barrier_semaphore()

    plane, place = lax.div(me, GROUP), lax.rem(me, GROUP)
    planes = band // GROUP
    places = [lax.rem(place + far_first(k, GROUP), GROUP) for k in range(GROUP)]
    my_levels = [lax.rem(my_lev + far_first(k, lev), lev) for k in range(lev)]

    def each_plane(act):
        def step(k, carry):
            odd = lax.rem(k, 2)
            ahead = planes // 2 + (1 - 2 * odd) * lax.div(k + 1, 2)
            base = lax.rem(plane + ahead, planes) * GROUP
            act(base, [base + p for p in places])
            return carry

        lax.fori_loop(0, planes - 1, step, 0)
        act(plane * GROUP, [plane * GROUP + p for p in places[:-1]])

    def greet(base, others):
        for other in others:
            pl.semaphore_signal(barrier, 1, device_id=(other, my_lev), device_id_type=pl.DeviceIdType.MESH)

    each_plane(greet)
    for i in range(1, lev):
        other = lax.rem(my_lev + i, lev)
        pl.semaphore_signal(barrier, 1, device_id=(me, other), device_id_type=pl.DeviceIdType.MESH)

    window = jnp.minimum(me * PER // LANES, PER * band // LANES - 2)
    pick_at = me * PER - window * LANES
    loads = [
        pltpu.make_async_copy(source, target, local_sem.at[i])
        for i, (source, target) in enumerate(
            (
                (column_hbm, column),
                (weight_hbm, weight),
                (winds_hbm, winds),
                (pick_hbm.at[:, pl.ds(pl.multiple_of(window * LANES, LANES), 2 * LANES)], pick),
                (coef_hbm, coef),
                (twiddle_hbm, twiddle),
                (inner_hbm, inner),
                (outer_hbm, outer),
                (wave_hbm, wave),
            )
        )
    ]
    for load in loads:
        load.start()

    def to_band(source, target, other, phase):
        return pltpu.make_async_remote_copy(
            src_ref=source,
            dst_ref=target,
            send_sem=send_sem.at[phase],
            recv_sem=recv_sem.at[phase],
            device_id=(other, my_lev),
            device_id_type=pl.DeviceIdType.MESH,
        )

    loads[0].wait()
    loads[1].wait()
    turned_column = column[...].astype(f32).T
    turned_weight = weight[...].T
    for h in range(2):
        request_out[pl.ds(h, band, stride=4), :] = turned_column[h * band : (h + 1) * band]
        request_out[pl.ds(2 + h, band, stride=4), :] = turned_weight[h * band : (h + 1) * band]
    loads[2].wait()
    blocks = winds.shape[0] // 3
    for a in range(3):
        part = winds[pl.ds(a * blocks, blocks), :]
        table[:, a, :] = part
        table[:, 4 + a, :] = part
    pl.semaphore_wait(barrier, band - 1 + lev - 1)
    mine = pltpu.make_async_copy(
        request_out.at[pl.ds(4 * me, 4)], request_in.at[pl.ds(4 * me, 4)], recv_sem.at[0]
    )
    mine.start()

    def send_request(base, others):
        for other in others:
            to_band(request_out.at[pl.ds(4 * other, 4)], request_in.at[pl.ds(4 * me, 4)], other, 0).start()

    each_plane(send_request)
    legendre_loads = [
        pltpu.make_async_copy(a_hbm, leg_a, legendre_sem.at[0]),
        pltpu.make_async_copy(b_hbm, leg_b, legendre_sem.at[1]),
    ]
    for load in legendre_loads:
        load.start()
    loads[3].wait()
    pltpu.make_async_copy(request_in, request_in, recv_sem.at[0]).wait()

    sub = lax.broadcasted_iota(jnp.int32, (8, LANES), 0)
    lane = lax.broadcasted_iota(jnp.int32, (8, LANES), 1)
    upper = sub < 4
    group = lane >> 5

    def weigh(other):
        rows = [jnp.broadcast_to(request_in[pl.ds(4 * other + k, 1), :], (8, LANES)) for k in range(4)]
        where = jnp.where(upper, rows[0], rows[1]).astype(jnp.int32)
        scale = jnp.where(upper, rows[2], rows[3])
        within, block = where & (BLK - 1), where >> 7
        total = jnp.zeros((8, LANES), f32)
        for c in range(PER):
            piece = table[pick[other, pick_at + c]]
            total = jnp.where(block == c, take(piece, within), total)
        return total * scale

    def fold_plane(base, totals):
        for p, total in enumerate(totals):
            taps[pl.ds(8 * p, 8), :] = total
        for r in range(0, 2 * GROUP, 8):
            x, y, z = (taps[pl.ds(4 * r + a, 8, stride=4), :] for a in range(3))
            x, y, z = (u + pltpu.roll(u, 64, 1) for u in (x, y, z))
            x = jnp.where(lane < 64, x, z)
            x, y = (u + pltpu.roll(u, 96, 1) for u in (x, y))
            reply_out[pl.ds(pl.multiple_of(2 * base, 8) + r, 8), :] = jnp.where(group == 1, y, jnp.where(group == 3, 0.0, x))

    def weigh_plane(base):
        return tuple(weigh(base + p) for p in range(GROUP))

    def send_reply(base, others):
        for other in others:
            to_band(reply_out.at[pl.ds(2 * other, 2)], reply_in.at[pl.ds(2 * me, 2)], other, 1).start()

    def base_of(k):
        ahead = planes // 2 + (1 - 2 * lax.rem(k, 2)) * lax.div(k + 1, 2)
        return lax.rem(plane + ahead, planes) * GROUP

    def reply(k, totals):
        following = weigh_plane(base_of(k + 1))
        fold_plane(base_of(k), totals)
        send_reply(base_of(k), [base_of(k) + p for p in places])
        return following

    totals = lax.fori_loop(0, planes - 1, reply, weigh_plane(base_of(0)))
    fold_plane(plane * GROUP, totals)
    send_reply(plane * GROUP, [plane * GROUP + p for p in places[:-1]])
    mine = pltpu.make_async_copy(
        reply_out.at[pl.ds(2 * me, 2)], reply_in.at[pl.ds(2 * me, 2)], recv_sem.at[1]
    )
    mine.start()
    for load in loads[4:]:
        load.wait()
    pltpu.make_async_copy(reply_in, reply_in, recv_sem.at[1]).wait()

    number = cycle_ref[0]
    odd = (jnp.full((2 * band, LANES), number, jnp.int32) & 1) == 1
    odd_thin = (jnp.full((2 * M // LANES, 4 * band), number, jnp.int32) & 1) == 1

    def by_parity(table, *at):
        return jnp.where(odd, table[(0, *at)], table[(1, *at)])

    cos_theta = 4.0 / 3.0 - 2.0 * jnp.full((2 * band, LANES), number, jnp.int32).astype(f32) / (3.0 * NSIDE)
    sin_theta = jnp.sqrt(1.0 - cos_theta * cos_theta)
    component = lax.broadcasted_iota(jnp.int32, (2 * band, LANES), 1) >> 5
    samples = reply_in[...]
    east = samples * by_parity(coef, 0)
    north = samples * jnp.where(component == 2, sin_theta, -cos_theta * by_parity(coef, 1))
    high, low = high_low(jnp.concatenate([east, north], 0))
    section = dot(high, inner[0]) + dot(low, inner[0]) + dot(high, inner[1])
    cos, sin = by_parity(twiddle, 0), by_parity(twiddle, 1)
    cos, sin = jnp.concatenate([cos, cos], 0), jnp.concatenate([sin, sin], 0)
    real, imag = section[:, :LANES], section[:, LANES:]
    real, imag = real * cos + imag * sin, imag * cos - real * sin
    n = 2 * band
    high, low = high_low(
        jnp.concatenate(
            [jnp.concatenate([real[:n], real[n:]], 1), jnp.concatenate([imag[:n], imag[n:]], 1)], 0
        )
    )
    outer_hi = jnp.where(odd_thin, outer[0, 0], outer[0, 1])
    outer_lo = jnp.where(odd_thin, outer[1, 0], outer[1, 1])
    full = dot(outer_hi, high) + dot(outer_hi, low) + dot(outer_lo, high)
    full = full.astype(bf16).astype(f32)
    rows = M // LANES
    for f, (r, c) in enumerate(((0, 0), (1, 0), (0, 1), (1, 1))):
        spectrum[pl.ds(f * rows, rows), :] = full[r * rows : (r + 1) * rows, c * LANES : (c + 1) * LANES]

    wave_row, wave_lane = wave[...] >> 7, wave[...] & (LANES - 1)
    field = (lane >> 3) & 3
    spot = (lane >> 5) * 8 + (lane & 7)
    for h in range(rows // 8):
        row_of, lane_of = wave_row[8 * h : 8 * h + 8], wave_lane[8 * h : 8 * h + 8]
        ordered = []
        for f in range(4):
            picked = jnp.zeros((8, LANES), f32)
            for r in range(rows):
                source = jnp.broadcast_to(spectrum[pl.ds(f * rows + r, 1), :], (8, LANES))
                picked = jnp.where(row_of == r, take(source, lane_of), picked)
            ordered.append(picked)
        for b in range(4):
            packed = jnp.zeros((8, LANES), f32)
            for f in range(4):
                packed = jnp.where(field == f, take(ordered[f], spot + 32 * b), packed)
            rows_out[pl.ds(32 * h + b, 8, stride=4), :] = packed

    def send_row(other, levels):
        for v in levels:
            pltpu.make_async_remote_copy(
                src_ref=rows_out.at[pl.ds(other, 1)],
                dst_ref=rows_in.at[pl.ds(my_lev * band + me, 1)],
                send_sem=send_sem.at[2],
                recv_sem=recv_sem.at[2],
                device_id=(other, v),
                device_id_type=pl.DeviceIdType.MESH,
            ).start()

    def send_rows(base, others):
        for other in others:
            send_row(other, my_levels)

    each_plane(send_rows)
    send_row(me, my_levels[:-1])
    mine = pltpu.make_async_copy(
        rows_out.at[pl.ds(me, 1)], rows_in.at[pl.ds(my_lev * band + me, 1)], recv_sem.at[2]
    )
    mine.start()
    pltpu.make_async_copy(rows_in, rows_in, recv_sem.at[2]).wait()

    level = lax.broadcasted_iota(jnp.int32, (band, LANES), 1) >> 5
    merged = jnp.zeros((band, LANES), f32)
    for v in range(lev):
        shifted = pltpu.roll(rows_in[pl.ds(v * band, band), :], lax.rem(v - my_lev + lev, lev) * 32, 1)
        merged = jnp.where(level == v, shifted, merged)
    turned = jnp.concatenate([merged, merged], 0).T
    first = lane < band
    sign_a, sign_b = (-1.0, 1.0, -1.0, 1.0), (-1.0, -1.0, 1.0, 1.0)

    def piece_of(v, f):
        return turned[(v * 4 + f) * 8 : (v * 4 + f) * 8 + 8]

    for o in range(4):
        for v in range(lev):
            out_ref[pl.ds((o * lev + v) * 8, 8), :] = jnp.where(
                first, sign_a[o] * piece_of(v, o ^ 1), sign_b[o] * piece_of(v, o ^ 2)
            )
    for load in legendre_loads:
        load.wait()
    pltpu.make_async_copy(request_out.at[pl.ds(0, 4 * (band - 1))], request_out.at[pl.ds(0, 4 * (band - 1))], send_sem.at[0]).wait()
    pltpu.make_async_copy(reply_out.at[pl.ds(0, 2 * (band - 1))], reply_out.at[pl.ds(0, 2 * (band - 1))], send_sem.at[1]).wait()
    sent = rows_in.at[pl.ds(0, lev * band - 1)]
    pltpu.make_async_copy(sent, sent, send_sem.at[2]).wait()


def legendre_kernel(wave_ref, left_ref, a_ref, b_ref, div_hbm, vort_hbm, div, vort, store_sem):
    me = lax.axis_index("band") * lax.axis_size("lev") + lax.axis_index("lev")
    owned, _, degrees = a_ref.shape
    half = left_ref.shape[0] // 2
    left = left_ref[...]
    slot = lax.broadcasted_iota(jnp.int32, left.shape, 0) % owned
    pieces = [jnp.where(slot == i, left, 0.0).astype(bf16) for i in range(owned)]
    pieces = [jnp.concatenate(pieces[i : i + 2], 1) for i in range(0, owned, 2)]
    row = lax.broadcasted_iota(jnp.int32, (owned, WIDTH), 0)
    lowest = jnp.zeros((owned, WIDTH), jnp.int32)
    for i in range(owned):
        lowest = jnp.where(row == i, wave_ref[me * owned + i], lowest)
    stores = []
    for j in range(degrees // WIDTH):
        at = pl.ds(j * WIDTH, WIDTH)
        total = jnp.zeros((2 * half, WIDTH), f32)
        for i in range(0, owned, 2):
            right = jnp.concatenate([a_ref[i, :, at], b_ref[i, :, at], a_ref[i + 1, :, at], b_ref[i + 1, :, at]], 0)
            total = total + dot(pieces[i // 2], right)
        keep = j * WIDTH + lax.broadcasted_iota(jnp.int32, (owned, WIDTH), 1) >= lowest
        for r in range(0, half, owned):
            div[r : r + owned, at] = jnp.where(keep, total[r : r + owned], 0.0)
            vort[r : r + owned, at] = jnp.where(keep, total[half + r : half + r + owned], 0.0)
        for k, (source, target) in enumerate(((div, div_hbm), (vort, vort_hbm))):
            stores.append(pltpu.make_async_copy(source.at[:, at], target.at[:, at], store_sem.at[2 * j + k]))
            stores[-1].start()
    for store in stores:
        store.wait()


def local(winds, remap_w, remap_col, block_pick, cycle_ids, wave_ids, legendre_a, legendre_b):
    band, lev = lax.axis_size("band"), lax.axis_size("lev")
    coef, twiddle, inner, outer = tables(band)
    columns = winds.shape[2]
    owned, cycles, degrees = legendre_a.shape
    blocks = columns // BLK
    hbm = pl.BlockSpec(memory_space=pltpu.HBM)
    smem = pl.BlockSpec(memory_space=pltpu.SMEM)
    vmem = pl.BlockSpec(memory_space=pltpu.VMEM)
    left, leg_a, leg_b = pl.pallas_call(
        functools.partial(modes_kernel, band, lev),
        out_shape=(
            pltpu.VMEM((4 * lev * owned, 2 * cycles), f32),
            pltpu.VMEM(legendre_a.shape, bf16),
            pltpu.VMEM(legendre_b.shape, bf16),
        ),
        in_specs=[smem] + [hbm] * 11,
        out_specs=(vmem, vmem, vmem),
        scratch_shapes=[
            pltpu.VMEM((3 * blocks, BLK), f32),
            pltpu.VMEM((2 * band, LANES), f32),
            pltpu.VMEM((2 * band, LANES), jnp.int32),
            pltpu.SMEM((band, 2 * LANES), jnp.int32),
            pltpu.VMEM((M // LANES, LANES), jnp.int32),
            pltpu.VMEM(coef.shape, f32),
            pltpu.VMEM(twiddle.shape, f32),
            pltpu.VMEM(inner.shape, bf16),
            pltpu.VMEM(outer.shape, bf16),
            pltpu.VMEM((blocks, 8, BLK), f32),
            pltpu.VMEM((4 * band, LANES), f32),
            pltpu.VMEM((4 * band, LANES), f32),
            pltpu.VMEM((8 * GROUP, LANES), f32),
            pltpu.VMEM((2 * band, LANES), f32),
            pltpu.VMEM((2 * band, LANES), f32),
            pltpu.VMEM((4 * M // LANES, LANES), f32),
            pltpu.VMEM((band, LANES), f32),
            pltpu.VMEM((lev * band, LANES), f32),
            pltpu.SemaphoreType.DMA((9,)),
            pltpu.SemaphoreType.DMA((3,)),
            pltpu.SemaphoreType.DMA((3,)),
            pltpu.SemaphoreType.DMA((2,)),
        ],
        compiler_params=pltpu.CompilerParams(collective_id=0, has_side_effects=True, vmem_limit_bytes=52 * 2**20),
        name="modes",
    )(
        cycle_ids,
        winds.reshape(3 * blocks, BLK),
        remap_w.reshape(2 * band, LANES),
        remap_col.reshape(2 * band, LANES),
        block_pick,
        wave_ids.reshape(M // LANES, LANES),
        coef,
        twiddle,
        inner,
        outer,
        legendre_a,
        legendre_b,
    )
    shape = jax.ShapeDtypeStruct((2 * lev * owned, degrees), f32)
    divergence, vorticity = pl.pallas_call(
        legendre_kernel,
        out_shape=(shape, shape),
        in_specs=[smem, vmem, vmem, vmem],
        out_specs=(hbm, hbm),
        scratch_shapes=[
            pltpu.VMEM(shape.shape, f32),
            pltpu.VMEM(shape.shape, f32),
            pltpu.SemaphoreType.DMA((2 * degrees // WIDTH,)),
        ],
        compiler_params=pltpu.CompilerParams(vmem_limit_bytes=32 * 2**20),
        name="legendre",
    )(wave_ids, left, leg_a, leg_b)
    whole = (2, lev, owned, degrees)
    return divergence.reshape(whole), vorticity.reshape(whole)


def solution(mesh):
    placed = (
        P(None, "lev", "band"),
        P(None, "band", None),
        P(None, "band", None),
        P(),
        P("band"),
        P(),
        P(("band", "lev"), None, None),
        P(("band", "lev"), None, None),
    )
    return jax.shard_map(
        local,
        mesh=mesh,
        in_specs=placed,
        out_specs=(P(None, None, ("band", "lev"), None), P(None, None, ("band", "lev"), None)),
        check_vma=False,
    )
```

```python
import functools
import math

import jax
import jax.numpy as jnp
import numpy as np
from jax import lax
from jax.experimental import pallas as pl
from jax.experimental.pallas import tpu as pltpu
from jax.sharding import PartitionSpec as P

NSIDE = 1024
NPHI = 4096
M = 2048
BLK = 128
PER = 12
TAPS = 4
LANES = 128
GROUP = 8
WIDTH = 512

f32 = jnp.float32
bf16 = jnp.bfloat16


def split(table):
    table = np.asarray(table, np.float32)
    high = table.astype(jnp.bfloat16)
    low = (table - high.astype(np.float32)).astype(jnp.bfloat16)
    return high, low


@functools.cache
def tables(band):
    rho = np.arange(2 * band)
    n = (rho % 2) * band + rho // 2
    b = np.arange(NPHI // (2 * band))
    mu = np.arange(LANES)
    m1 = np.arange(M // LANES)
    turn = 2.0 * np.pi / NPHI
    coef, twiddle, outer_hi, outer_lo = [], [], [], []
    for half in (0, 1):
        delta = 1.0 - 0.5 * half
        azimuth = turn * (2 * band * b[None, :] + n[:, None] + delta)
        zero = np.zeros_like(azimuth)
        cos, sin = np.cos(azimuth), np.sin(azimuth)
        coef.append(np.stack([np.concatenate([-sin, cos, zero, zero], 1), np.concatenate([cos, sin, zero, zero], 1)]))
        phi = turn * mu[None, :] * (n[:, None] + delta)
        twiddle.append(np.stack([np.cos(phi), np.sin(phi)]))
        psi = turn * LANES * m1[:, None] * (n[None, :] + delta)
        full = np.concatenate(
            [np.concatenate([np.cos(psi), np.sin(psi)], 1), np.concatenate([-np.sin(psi), np.cos(psi)], 1)], 0
        )
        high, low = split(full)
        outer_hi.append(high)
        outer_lo.append(low)
    angle = 2.0 * np.pi / b.size * (b[:, None] * mu[None, :])
    inner = np.tile(np.concatenate([np.cos(angle), -np.sin(angle)], 1), (4, 1))
    inner_hi, inner_lo = split(inner)
    return (
        np.stack(coef).astype(np.float32),
        np.stack(twiddle).astype(np.float32),
        np.stack([inner_hi, inner_lo]),
        np.stack([np.stack(outer_hi), np.stack(outer_lo)]),
    )


def dot(a, b):
    return jnp.dot(a, b, preferred_element_type=f32)


def far_first(i, count):
    return count // 2 + (1 - 2 * (i % 2)) * ((i + 1) // 2)


def high_low(x):
    high = x.astype(bf16)
    return high, (x - high.astype(f32)).astype(bf16)


def take(x, index):
    return jnp.take_along_axis(x, index, axis=1, mode="promise_in_bounds")


def modes_kernel(
    band,
    lev,
    cycle_ref,
    winds_hbm,
    weight_hbm,
    column_hbm,
    pick_hbm,
    wave_hbm,
    coef_hbm,
    twiddle_hbm,
    inner_hbm,
    outer_hbm,
    a_hbm,
    b_hbm,
    out_ref,
    lowest_ref,
    leg_a,
    leg_b,
    winds,
    weight,
    column,
    pick,
    wave,
    coef,
    twiddle,
    inner,
    outer,
    table,
    request_out,
    request_in,
    taps,
    reply_out,
    reply_in,
    spectrum,
    rows_out,
    rows_in,
    local_sem,
    send_sem,
    recv_sem,
    legendre_sem,
):
    me = lax.axis_index("band")
    my_lev = lax.axis_index("lev")
    barrier = pltpu.get_barrier_semaphore()

    plane, place = lax.div(me, GROUP), lax.rem(me, GROUP)
    planes = band // GROUP
    places = [lax.rem(place + far_first(k, GROUP), GROUP) for k in range(GROUP)]
    my_levels = [lax.rem(my_lev + far_first(k, lev), lev) for k in range(lev)]

    def each_plane(act):
        def step(k, carry):
            odd = lax.rem(k, 2)
            ahead = planes // 2 + (1 - 2 * odd) * lax.div(k + 1, 2)
            base = lax.rem(plane + ahead, planes) * GROUP
            act(base, [base + p for p in places])
            return carry

        lax.fori_loop(0, planes - 1, step, 0)
        act(plane * GROUP, [plane * GROUP + p for p in places[:-1]])

    def greet(base, others):
        for other in others:
            pl.semaphore_signal(barrier, 1, device_id=(other, my_lev), device_id_type=pl.DeviceIdType.MESH)

    each_plane(greet)
    for i in range(1, lev):
        other = lax.rem(my_lev + i, lev)
        pl.semaphore_signal(barrier, 1, device_id=(me, other), device_id_type=pl.DeviceIdType.MESH)

    window = jnp.minimum(me * PER // LANES, PER * band // LANES - 2)
    pick_at = me * PER - window * LANES
    loads = [
        pltpu.make_async_copy(source, target, local_sem.at[i])
        for i, (source, target) in enumerate(
            (
                (column_hbm, column),
                (weight_hbm, weight),
                (winds_hbm, winds),
                (pick_hbm.at[:, pl.ds(pl.multiple_of(window * LANES, LANES), 2 * LANES)], pick),
                (coef_hbm, coef),
                (twiddle_hbm, twiddle),
                (inner_hbm, inner),
                (outer_hbm, outer),
                (wave_hbm, wave),
            )
        )
    ]
    for load in loads:
        load.start()

    def to_band(source, target, other, phase):
        return pltpu.make_async_remote_copy(
            src_ref=source,
            dst_ref=target,
            send_sem=send_sem.at[phase],
            recv_sem=recv_sem.at[phase],
            device_id=(other, my_lev),
            device_id_type=pl.DeviceIdType.MESH,
        )

    loads[0].wait()
    loads[1].wait()
    turned_column = column[...].astype(f32).T
    turned_weight = weight[...].T
    for h in range(2):
        request_out[pl.ds(h, band, stride=4), :] = turned_column[h * band : (h + 1) * band]
        request_out[pl.ds(2 + h, band, stride=4), :] = turned_weight[h * band : (h + 1) * band]
    loads[2].wait()
    blocks = winds.shape[0] // 3
    for a in range(3):
        part = winds[pl.ds(a * blocks, blocks), :]
        table[:, a, :] = part
        table[:, 4 + a, :] = part
    pl.semaphore_wait(barrier, band - 1 + lev - 1)
    mine = pltpu.make_async_copy(
        request_out.at[pl.ds(4 * me, 4)], request_in.at[pl.ds(4 * me, 4)], recv_sem.at[0]
    )
    mine.start()

    def send_request(base, others):
        for other in others:
            to_band(request_out.at[pl.ds(4 * other, 4)], request_in.at[pl.ds(4 * me, 4)], other, 0).start()

    each_plane(send_request)
    legendre_loads = [
        pltpu.make_async_copy(a_hbm, leg_a, legendre_sem.at[0]),
        pltpu.make_async_copy(b_hbm, leg_b, legendre_sem.at[1]),
    ]
    for load in legendre_loads:
        load.start()
    sub = lax.broadcasted_iota(jnp.int32, (8, LANES), 0)
    lane = lax.broadcasted_iota(jnp.int32, (8, LANES), 1)
    loads[8].wait()
    slots = out_ref.shape[0] // (4 * lev)
    first_slot = (me * lev + my_lev) * slots
    near = jnp.broadcast_to(wave[pl.ds(lax.div(first_slot, LANES), 1), :], (slots, LANES))
    own = lane == sub + lax.rem(first_slot, LANES)
    lowest_ref[...] = jnp.broadcast_to(jnp.sum(jnp.where(own, near, 0), 1, keepdims=True), (slots, LANES))

    loads[3].wait()
    pltpu.make_async_copy(request_in, request_in, recv_sem.at[0]).wait()

    upper = sub < 4
    group = lane >> 5

    def weigh(other):
        rows = [jnp.broadcast_to(request_in[pl.ds(4 * other + k, 1), :], (8, LANES)) for k in range(4)]
        where = jnp.where(upper, rows[0], rows[1]).astype(jnp.int32)
        scale = jnp.where(upper, rows[2], rows[3])
        within, block = where & (BLK - 1), where >> 7
        total = jnp.zeros((8, LANES), f32)
        for c in range(PER):
            piece = table[pick[other, pick_at + c]]
            total = jnp.where(block == c, take(piece, within), total)
        return total * scale

    def fold_plane(base, totals):
        for p, total in enumerate(totals):
            taps[pl.ds(8 * p, 8), :] = total
        for r in range(0, 2 * GROUP, 8):
            x, y, z = (taps[pl.ds(4 * r + a, 8, stride=4), :] for a in range(3))
            x, y, z = (u + pltpu.roll(u, 64, 1) for u in (x, y, z))
            x = jnp.where(lane < 64, x, z)
            x, y = (u + pltpu.roll(u, 96, 1) for u in (x, y))
            reply_out[pl.ds(pl.multiple_of(2 * base, 8) + r, 8), :] = jnp.where(group == 1, y, jnp.where(group == 3, 0.0, x))

    def weigh_plane(base):
        return tuple(weigh(base + p) for p in range(GROUP))

    def send_reply(base, others):
        for other in others:
            to_band(reply_out.at[pl.ds(2 * other, 2)], reply_in.at[pl.ds(2 * me, 2)], other, 1).start()

    def base_of(k):
        ahead = planes // 2 + (1 - 2 * lax.rem(k, 2)) * lax.div(k + 1, 2)
        return lax.rem(plane + ahead, planes) * GROUP

    def reply(k, totals):
        following = weigh_plane(base_of(k + 1))
        fold_plane(base_of(k), totals)
        send_reply(base_of(k), [base_of(k) + p for p in places])
        return following

    totals = lax.fori_loop(0, planes - 1, reply, weigh_plane(base_of(0)))
    fold_plane(plane * GROUP, totals)
    send_reply(plane * GROUP, [plane * GROUP + p for p in places[:-1]])
    mine = pltpu.make_async_copy(
        reply_out.at[pl.ds(2 * me, 2)], reply_in.at[pl.ds(2 * me, 2)], recv_sem.at[1]
    )
    mine.start()
    for load in loads[4:8]:
        load.wait()
    pltpu.make_async_copy(reply_in, reply_in, recv_sem.at[1]).wait()

    number = cycle_ref[0]
    odd = (jnp.full((2 * band, LANES), number, jnp.int32) & 1) == 1
    odd_thin = (jnp.full((2 * M // LANES, 4 * band), number, jnp.int32) & 1) == 1

    def by_parity(table, *at):
        return jnp.where(odd, table[(0, *at)], table[(1, *at)])

    cos_theta = 4.0 / 3.0 - 2.0 * jnp.full((2 * band, LANES), number, jnp.int32).astype(f32) / (3.0 * NSIDE)
    sin_theta = jnp.sqrt(1.0 - cos_theta * cos_theta)
    component = lax.broadcasted_iota(jnp.int32, (2 * band, LANES), 1) >> 5
    samples = reply_in[...]
    east = samples * by_parity(coef, 0)
    north = samples * jnp.where(component == 2, sin_theta, -cos_theta * by_parity(coef, 1))
    high, low = high_low(jnp.concatenate([east, north], 0))
    section = dot(high, inner[0]) + dot(low, inner[0]) + dot(high, inner[1])
    cos, sin = by_parity(twiddle, 0), by_parity(twiddle, 1)
    cos, sin = jnp.concatenate([cos, cos], 0), jnp.concatenate([sin, sin], 0)
    real, imag = section[:, :LANES], section[:, LANES:]
    real, imag = real * cos + imag * sin, imag * cos - real * sin
    n = 2 * band
    high, low = high_low(
        jnp.concatenate(
            [jnp.concatenate([real[:n], real[n:]], 1), jnp.concatenate([imag[:n], imag[n:]], 1)], 0
        )
    )
    outer_hi = jnp.where(odd_thin, outer[0, 0], outer[0, 1])
    outer_lo = jnp.where(odd_thin, outer[1, 0], outer[1, 1])
    full = dot(outer_hi, high) + dot(outer_hi, low) + dot(outer_lo, high)
    full = full.astype(bf16).astype(f32)
    rows = M // LANES
    for f, (r, c) in enumerate(((0, 0), (1, 0), (0, 1), (1, 1))):
        spectrum[pl.ds(f * rows, rows), :] = full[r * rows : (r + 1) * rows, c * LANES : (c + 1) * LANES]

    wave_row, wave_lane = wave[...] >> 7, wave[...] & (LANES - 1)
    field = (lane >> 3) & 3
    spot = (lane >> 5) * 8 + (lane & 7)
    for h in range(rows // 8):
        row_of, lane_of = wave_row[8 * h : 8 * h + 8], wave_lane[8 * h : 8 * h + 8]
        ordered = []
        for f in range(4):
            picked = jnp.zeros((8, LANES), f32)
            for r in range(rows):
                source = jnp.broadcast_to(spectrum[pl.ds(f * rows + r, 1), :], (8, LANES))
                picked = jnp.where(row_of == r, take(source, lane_of), picked)
            ordered.append(picked)
        for b in range(4):
            packed = jnp.zeros((8, LANES), f32)
            for f in range(4):
                packed = jnp.where(field == f, take(ordered[f], spot + 32 * b), packed)
            rows_out[pl.ds(32 * h + b, 8, stride=4), :] = packed

    def send_row(other, levels):
        for v in levels:
            pltpu.make_async_remote_copy(
                src_ref=rows_out.at[pl.ds(other, 1)],
                dst_ref=rows_in.at[pl.ds(my_lev * band + me, 1)],
                send_sem=send_sem.at[2],
                recv_sem=recv_sem.at[2],
                device_id=(other, v),
                device_id_type=pl.DeviceIdType.MESH,
            ).start()

    def send_rows(base, others):
        for other in others:
            send_row(other, my_levels)

    each_plane(send_rows)
    send_row(me, my_levels[:-1])
    mine = pltpu.make_async_copy(
        rows_out.at[pl.ds(me, 1)], rows_in.at[pl.ds(my_lev * band + me, 1)], recv_sem.at[2]
    )
    mine.start()
    pltpu.make_async_copy(rows_in, rows_in, recv_sem.at[2]).wait()

    level = lax.broadcasted_iota(jnp.int32, (band, LANES), 1) >> 5
    merged = jnp.zeros((band, LANES), f32)
    for v in range(lev):
        shifted = pltpu.roll(rows_in[pl.ds(v * band, band), :], lax.rem(v - my_lev + lev, lev) * 32, 1)
        merged = jnp.where(level == v, shifted, merged)
    turned = jnp.concatenate([merged, merged], 0).T
    first = lane < band
    sign_a, sign_b = (-1.0, 1.0, -1.0, 1.0), (-1.0, -1.0, 1.0, 1.0)

    def piece_of(v, f):
        return turned[(v * 4 + f) * 8 : (v * 4 + f) * 8 + 8]

    for o in range(4):
        for v in range(lev):
            out_ref[pl.ds((o * lev + v) * 8, 8), :] = jnp.where(
                first, sign_a[o] * piece_of(v, o ^ 1), sign_b[o] * piece_of(v, o ^ 2)
            )
    for load in legendre_loads:
        load.wait()
    pltpu.make_async_copy(request_out.at[pl.ds(0, 4 * (band - 1))], request_out.at[pl.ds(0, 4 * (band - 1))], send_sem.at[0]).wait()
    pltpu.make_async_copy(reply_out.at[pl.ds(0, 2 * (band - 1))], reply_out.at[pl.ds(0, 2 * (band - 1))], send_sem.at[1]).wait()
    sent = rows_in.at[pl.ds(0, lev * band - 1)]
    pltpu.make_async_copy(sent, sent, send_sem.at[2]).wait()


def legendre_kernel(lowest_ref, left_ref, a_ref, b_ref, div_hbm, vort_hbm, div, vort, store_sem):
    owned, _, degrees = a_ref.shape
    half = left_ref.shape[0] // 2
    left = left_ref[...]
    slot = lax.broadcasted_iota(jnp.int32, left.shape, 0) % owned
    pieces = [jnp.where(slot == i, left, 0.0).astype(bf16) for i in range(owned)]
    pieces = [jnp.concatenate(pieces[i : i + 2], 1) for i in range(0, owned, 2)]
    lowest = jnp.concatenate([lowest_ref[...]] * (WIDTH // LANES), 1)
    stores = []
    for j in range(degrees // WIDTH):
        at = pl.ds(j * WIDTH, WIDTH)
        total = jnp.zeros((2 * half, WIDTH), f32)
        for i in range(0, owned, 2):
            right = jnp.concatenate([a_ref[i, :, at], b_ref[i, :, at], a_ref[i + 1, :, at], b_ref[i + 1, :, at]], 0)
            total = total + dot(pieces[i // 2], right)
        keep = j * WIDTH + lax.broadcasted_iota(jnp.int32, (owned, WIDTH), 1) >= lowest
        for r in range(0, half, owned):
            div[r : r + owned, at] = jnp.where(keep, total[r : r + owned], 0.0)
            vort[r : r + owned, at] = jnp.where(keep, total[half + r : half + r + owned], 0.0)
        for k, (source, target) in enumerate(((div, div_hbm), (vort, vort_hbm))):
            stores.append(pltpu.make_async_copy(source.at[:, at], target.at[:, at], store_sem.at[2 * j + k]))
            stores[-1].start()
    for store in stores:
        store.wait()


def local(winds, remap_w, remap_col, block_pick, cycle_ids, wave_ids, legendre_a, legendre_b):
    band, lev = lax.axis_size("band"), lax.axis_size("lev")
    coef, twiddle, inner, outer = tables(band)
    columns = winds.shape[2]
    owned, cycles, degrees = legendre_a.shape
    blocks = columns // BLK
    hbm = pl.BlockSpec(memory_space=pltpu.HBM)
    smem = pl.BlockSpec(memory_space=pltpu.SMEM)
    vmem = pl.BlockSpec(memory_space=pltpu.VMEM)
    left, lowest, leg_a, leg_b = pl.pallas_call(
        functools.partial(modes_kernel, band, lev),
        out_shape=(
            pltpu.VMEM((4 * lev * owned, 2 * cycles), f32),
            pltpu.VMEM((owned, LANES), jnp.int32),
            pltpu.VMEM(legendre_a.shape, bf16),
            pltpu.VMEM(legendre_b.shape, bf16),
        ),
        in_specs=[smem] + [hbm] * 11,
        out_specs=(vmem, vmem, vmem, vmem),
        scratch_shapes=[
            pltpu.VMEM((3 * blocks, BLK), f32),
            pltpu.VMEM((2 * band, LANES), f32),
            pltpu.VMEM((2 * band, LANES), jnp.int32),
            pltpu.SMEM((band, 2 * LANES), jnp.int32),
            pltpu.VMEM((M // LANES, LANES), jnp.int32),
            pltpu.VMEM(coef.shape, f32),
            pltpu.VMEM(twiddle.shape, f32),
            pltpu.VMEM(inner.shape, bf16),
            pltpu.VMEM(outer.shape, bf16),
            pltpu.VMEM((blocks, 8, BLK), f32),
            pltpu.VMEM((4 * band, LANES), f32),
            pltpu.VMEM((4 * band, LANES), f32),
            pltpu.VMEM((8 * GROUP, LANES), f32),
            pltpu.VMEM((2 * band, LANES), f32),
            pltpu.VMEM((2 * band, LANES), f32),
            pltpu.VMEM((4 * M // LANES, LANES), f32),
            pltpu.VMEM((band, LANES), f32),
            pltpu.VMEM((lev * band, LANES), f32),
            pltpu.SemaphoreType.DMA((9,)),
            pltpu.SemaphoreType.DMA((3,)),
            pltpu.SemaphoreType.DMA((3,)),
            pltpu.SemaphoreType.DMA((2,)),
        ],
        compiler_params=pltpu.CompilerParams(collective_id=0, has_side_effects=True, vmem_limit_bytes=52 * 2**20),
        name="modes",
    )(
        cycle_ids,
        winds.reshape(3 * blocks, BLK),
        remap_w.reshape(2 * band, LANES),
        remap_col.reshape(2 * band, LANES),
        block_pick,
        wave_ids.reshape(M // LANES, LANES),
        coef,
        twiddle,
        inner,
        outer,
        legendre_a,
        legendre_b,
    )
    shape = jax.ShapeDtypeStruct((2 * lev * owned, degrees), f32)
    divergence, vorticity = pl.pallas_call(
        legendre_kernel,
        out_shape=(shape, shape),
        in_specs=[vmem, vmem, vmem, vmem],
        out_specs=(hbm, hbm),
        scratch_shapes=[
            pltpu.VMEM(shape.shape, f32),
            pltpu.VMEM(shape.shape, f32),
            pltpu.SemaphoreType.DMA((2 * degrees // WIDTH,)),
        ],
        compiler_params=pltpu.CompilerParams(vmem_limit_bytes=32 * 2**20),
        name="legendre",
    )(lowest, left, leg_a, leg_b)
    whole = (2, lev, owned, degrees)
    return divergence.reshape(whole), vorticity.reshape(whole)


def solution(mesh):
    placed = (
        P(None, "lev", "band"),
        P(None, "band", None),
        P(None, "band", None),
        P(),
        P("band"),
        P(),
        P(("band", "lev"), None, None),
        P(("band", "lev"), None, None),
    )
    return jax.shard_map(
        local,
        mesh=mesh,
        in_specs=placed,
        out_specs=(P(None, None, ("band", "lev"), None), P(None, None, ("band", "lev"), None)),
        check_vma=False,
    )
```

```python
import functools
import math

import jax
import jax.numpy as jnp
import numpy as np
from jax import lax
from jax.experimental import pallas as pl
from jax.experimental.pallas import tpu as pltpu
from jax.sharding import PartitionSpec as P

NSIDE = 1024
NPHI = 4096
M = 2048
BLK = 128
PER = 12
TAPS = 4
LANES = 128
GROUP = 8
WIDTH = 512

f32 = jnp.float32
bf16 = jnp.bfloat16


def split(table):
    table = np.asarray(table, np.float32)
    high = table.astype(jnp.bfloat16)
    low = (table - high.astype(np.float32)).astype(jnp.bfloat16)
    return high, low


@functools.cache
def tables(band):
    rho = np.arange(2 * band)
    n = (rho % 2) * band + rho // 2
    b = np.arange(NPHI // (2 * band))
    mu = np.arange(LANES)
    m1 = np.arange(M // LANES)
    turn = 2.0 * np.pi / NPHI
    coef, twiddle, outer_hi, outer_lo = [], [], [], []
    for half in (0, 1):
        delta = 1.0 - 0.5 * half
        azimuth = turn * (2 * band * b[None, :] + n[:, None] + delta)
        zero = np.zeros_like(azimuth)
        cos, sin = np.cos(azimuth), np.sin(azimuth)
        coef.append(np.stack([np.concatenate([-sin, cos, zero, zero], 1), np.concatenate([cos, sin, zero, zero], 1)]))
        phi = turn * mu[None, :] * (n[:, None] + delta)
        twiddle.append(np.stack([np.cos(phi), np.sin(phi)]))
        psi = turn * LANES * m1[:, None] * (n[None, :] + delta)
        full = np.concatenate(
            [np.concatenate([np.cos(psi), np.sin(psi)], 1), np.concatenate([-np.sin(psi), np.cos(psi)], 1)], 0
        )
        high, low = split(full)
        outer_hi.append(high)
        outer_lo.append(low)
    angle = 2.0 * np.pi / b.size * (b[:, None] * mu[None, :])
    inner = np.tile(np.concatenate([np.cos(angle), -np.sin(angle)], 1), (4, 1))
    inner_hi, inner_lo = split(inner)
    return (
        np.stack(coef).astype(np.float32),
        np.stack(twiddle).astype(np.float32),
        np.stack([inner_hi, inner_lo]),
        np.stack([np.stack(outer_hi), np.stack(outer_lo)]),
    )


def dot(a, b):
    return jnp.dot(a, b, preferred_element_type=f32)


def far_first(i, count):
    return count // 2 + (1 - 2 * (i % 2)) * ((i + 1) // 2)


def high_low(x):
    high = x.astype(bf16)
    return high, (x - high.astype(f32)).astype(bf16)


def take(x, index):
    return jnp.take_along_axis(x, index, axis=1, mode="promise_in_bounds")


def modes_kernel(
    band,
    lev,
    cycle_ref,
    winds_hbm,
    weight_hbm,
    column_hbm,
    pick_hbm,
    wave_hbm,
    coef_hbm,
    twiddle_hbm,
    inner_hbm,
    outer_hbm,
    a_hbm,
    b_hbm,
    out_ref,
    lowest_ref,
    leg_a,
    leg_b,
    winds,
    weight,
    column,
    pick_window,
    pick_rows,
    pick,
    wave,
    coef,
    twiddle,
    inner,
    outer,
    table,
    request_out,
    request_in,
    taps,
    reply_out,
    reply_in,
    spectrum,
    rows_out,
    rows_in,
    local_sem,
    send_sem,
    recv_sem,
    legendre_sem,
):
    me = lax.axis_index("band")
    my_lev = lax.axis_index("lev")
    barrier = pltpu.get_barrier_semaphore()

    plane, place = lax.div(me, GROUP), lax.rem(me, GROUP)
    planes = band // GROUP
    places = [lax.rem(place + far_first(k, GROUP), GROUP) for k in range(GROUP)]
    my_levels = [lax.rem(my_lev + far_first(k, lev), lev) for k in range(lev)]

    def each_plane(act):
        def step(k, carry):
            odd = lax.rem(k, 2)
            ahead = planes // 2 + (1 - 2 * odd) * lax.div(k + 1, 2)
            base = lax.rem(plane + ahead, planes) * GROUP
            act(base, [base + p for p in places])
            return carry

        lax.fori_loop(0, planes - 1, step, 0)
        act(plane * GROUP, [plane * GROUP + p for p in places[:-1]])

    def greet(base, others):
        for other in others:
            pl.semaphore_signal(barrier, 1, device_id=(other, my_lev), device_id_type=pl.DeviceIdType.MESH)

    each_plane(greet)
    for i in range(1, lev):
        other = lax.rem(my_lev + i, lev)
        pl.semaphore_signal(barrier, 1, device_id=(me, other), device_id_type=pl.DeviceIdType.MESH)

    window = jnp.minimum(me * PER // LANES, PER * band // LANES - 2)
    pick_at = me * PER - window * LANES
    loads = [
        pltpu.make_async_copy(source, target, local_sem.at[i])
        for i, (source, target) in enumerate(
            (
                (column_hbm, column),
                (weight_hbm, weight),
                (winds_hbm, winds),
                (pick_hbm.at[:, pl.ds(pl.multiple_of(window * LANES, LANES), 2 * LANES)], pick_window),
                (coef_hbm, coef),
                (twiddle_hbm, twiddle),
                (inner_hbm, inner),
                (outer_hbm, outer),
                (wave_hbm, wave),
            )
        )
    ]
    for load in loads:
        load.start()

    def to_band(source, target, other, phase):
        return pltpu.make_async_remote_copy(
            src_ref=source,
            dst_ref=target,
            send_sem=send_sem.at[phase],
            recv_sem=recv_sem.at[phase],
            device_id=(other, my_lev),
            device_id_type=pl.DeviceIdType.MESH,
        )

    loads[0].wait()
    loads[1].wait()
    turned_column = column[...].astype(f32).T
    turned_weight = weight[...].T
    for h in range(2):
        request_out[pl.ds(h, band, stride=4), :] = turned_column[h * band : (h + 1) * band]
        request_out[pl.ds(2 + h, band, stride=4), :] = turned_weight[h * band : (h + 1) * band]
    loads[2].wait()
    blocks = winds.shape[0] // 3
    for a in range(3):
        part = winds[pl.ds(a * blocks, blocks), :]
        table[:, a, :] = part
        table[:, 4 + a, :] = part
    loads[3].wait()
    pick_rows[...] = pltpu.roll(pick_window[...], lax.rem(2 * LANES - pick_at, 2 * LANES), 1)[:, :LANES]
    pick_load = pltpu.make_async_copy(pick_rows, pick, local_sem.at[9])
    pick_load.start()
    pl.semaphore_wait(barrier, band - 1 + lev - 1)
    mine = pltpu.make_async_copy(
        request_out.at[pl.ds(4 * me, 4)], request_in.at[pl.ds(4 * me, 4)], recv_sem.at[0]
    )
    mine.start()

    def send_request(base, others):
        for other in others:
            to_band(request_out.at[pl.ds(4 * other, 4)], request_in.at[pl.ds(4 * me, 4)], other, 0).start()

    each_plane(send_request)
    legendre_loads = [
        pltpu.make_async_copy(a_hbm, leg_a, legendre_sem.at[0]),
        pltpu.make_async_copy(b_hbm, leg_b, legendre_sem.at[1]),
    ]
    for load in legendre_loads:
        load.start()
    sub = lax.broadcasted_iota(jnp.int32, (8, LANES), 0)
    lane = lax.broadcasted_iota(jnp.int32, (8, LANES), 1)
    loads[8].wait()
    slots = out_ref.shape[0] // (4 * lev)
    first_slot = (me * lev + my_lev) * slots
    near = jnp.broadcast_to(wave[pl.ds(lax.div(first_slot, LANES), 1), :], (slots, LANES))
    own = lane == sub + lax.rem(first_slot, LANES)
    lowest_ref[...] = jnp.broadcast_to(jnp.sum(jnp.where(own, near, 0), 1, keepdims=True), (slots, LANES))

    pick_load.wait()
    pltpu.make_async_copy(request_in, request_in, recv_sem.at[0]).wait()

    upper = sub < 4
    group = lane >> 5

    def weigh(other):
        rows = [jnp.broadcast_to(request_in[pl.ds(4 * other + k, 1), :], (8, LANES)) for k in range(4)]
        where = jnp.where(upper, rows[0], rows[1]).astype(jnp.int32)
        scale = jnp.where(upper, rows[2], rows[3])
        within, block = where & (BLK - 1), where >> 7
        total = jnp.zeros((8, LANES), f32)
        for c in range(PER):
            piece = table[pick[other, c]]
            total = jnp.where(block == c, take(piece, within), total)
        return total * scale

    def fold_plane(base, totals):
        for p, total in enumerate(totals):
            taps[pl.ds(8 * p, 8), :] = total
        for r in range(0, 2 * GROUP, 8):
            x, y, z = (taps[pl.ds(4 * r + a, 8, stride=4), :] for a in range(3))
            x, y, z = (u + pltpu.roll(u, 64, 1) for u in (x, y, z))
            x = jnp.where(lane < 64, x, z)
            x, y = (u + pltpu.roll(u, 96, 1) for u in (x, y))
            reply_out[pl.ds(pl.multiple_of(2 * base, 8) + r, 8), :] = jnp.where(group == 1, y, jnp.where(group == 3, 0.0, x))

    def weigh_plane(base):
        return tuple(weigh(base + p) for p in range(GROUP))

    def send_reply(base, others):
        for other in others:
            to_band(reply_out.at[pl.ds(2 * other, 2)], reply_in.at[pl.ds(2 * me, 2)], other, 1).start()

    def base_of(k):
        ahead = planes // 2 + (1 - 2 * lax.rem(k, 2)) * lax.div(k + 1, 2)
        return lax.rem(plane + ahead, planes) * GROUP

    def reply(k, totals):
        following = weigh_plane(base_of(k + 1))
        fold_plane(base_of(k), totals)
        send_reply(base_of(k), [base_of(k) + p for p in places])
        return following

    totals = lax.fori_loop(0, planes - 1, reply, weigh_plane(base_of(0)))
    fold_plane(plane * GROUP, totals)
    send_reply(plane * GROUP, [plane * GROUP + p for p in places[:-1]])
    mine = pltpu.make_async_copy(
        reply_out.at[pl.ds(2 * me, 2)], reply_in.at[pl.ds(2 * me, 2)], recv_sem.at[1]
    )
    mine.start()
    for load in loads[4:8]:
        load.wait()
    pltpu.make_async_copy(reply_in, reply_in, recv_sem.at[1]).wait()

    number = cycle_ref[0]
    odd = (jnp.full((2 * band, LANES), number, jnp.int32) & 1) == 1
    odd_thin = (jnp.full((2 * M // LANES, 4 * band), number, jnp.int32) & 1) == 1

    def by_parity(table, *at):
        return jnp.where(odd, table[(0, *at)], table[(1, *at)])

    cos_theta = 4.0 / 3.0 - 2.0 * jnp.full((2 * band, LANES), number, jnp.int32).astype(f32) / (3.0 * NSIDE)
    sin_theta = jnp.sqrt(1.0 - cos_theta * cos_theta)
    component = lax.broadcasted_iota(jnp.int32, (2 * band, LANES), 1) >> 5
    samples = reply_in[...]
    east = samples * by_parity(coef, 0)
    north = samples * jnp.where(component == 2, sin_theta, -cos_theta * by_parity(coef, 1))
    high, low = high_low(jnp.concatenate([east, north], 0))
    section = dot(high, inner[0]) + dot(low, inner[0]) + dot(high, inner[1])
    cos, sin = by_parity(twiddle, 0), by_parity(twiddle, 1)
    cos, sin = jnp.concatenate([cos, cos], 0), jnp.concatenate([sin, sin], 0)
    real, imag = section[:, :LANES], section[:, LANES:]
    real, imag = real * cos + imag * sin, imag * cos - real * sin
    n = 2 * band
    high, low = high_low(
        jnp.concatenate(
            [jnp.concatenate([real[:n], real[n:]], 1), jnp.concatenate([imag[:n], imag[n:]], 1)], 0
        )
    )
    outer_hi = jnp.where(odd_thin, outer[0, 0], outer[0, 1])
    outer_lo = jnp.where(odd_thin, outer[1, 0], outer[1, 1])
    full = dot(outer_hi, high) + dot(outer_hi, low) + dot(outer_lo, high)
    full = full.astype(bf16).astype(f32)
    rows = M // LANES
    for f, (r, c) in enumerate(((0, 0), (1, 0), (0, 1), (1, 1))):
        spectrum[pl.ds(f * rows, rows), :] = full[r * rows : (r + 1) * rows, c * LANES : (c + 1) * LANES]

    wave_row, wave_lane = wave[...] >> 7, wave[...] & (LANES - 1)
    field = (lane >> 3) & 3
    spot = (lane >> 5) * 8 + (lane & 7)
    for h in range(rows // 8):
        row_of, lane_of = wave_row[8 * h : 8 * h + 8], wave_lane[8 * h : 8 * h + 8]
        ordered = []
        for f in range(4):
            picked = jnp.zeros((8, LANES), f32)
            for r in range(rows):
                source = jnp.broadcast_to(spectrum[pl.ds(f * rows + r, 1), :], (8, LANES))
                picked = jnp.where(row_of == r, take(source, lane_of), picked)
            ordered.append(picked)
        for b in range(4):
            packed = jnp.zeros((8, LANES), f32)
            for f in range(4):
                packed = jnp.where(field == f, take(ordered[f], spot + 32 * b), packed)
            rows_out[pl.ds(32 * h + b, 8, stride=4), :] = packed

    def send_row(other, levels):
        for v in levels:
            pltpu.make_async_remote_copy(
                src_ref=rows_out.at[pl.ds(other, 1)],
                dst_ref=rows_in.at[pl.ds(my_lev * band + me, 1)],
                send_sem=send_sem.at[2],
                recv_sem=recv_sem.at[2],
                device_id=(other, v),
                device_id_type=pl.DeviceIdType.MESH,
            ).start()

    def send_rows(base, others):
        for other in others:
            send_row(other, my_levels)

    each_plane(send_rows)
    send_row(me, my_levels[:-1])
    mine = pltpu.make_async_copy(
        rows_out.at[pl.ds(me, 1)], rows_in.at[pl.ds(my_lev * band + me, 1)], recv_sem.at[2]
    )
    mine.start()
    pltpu.make_async_copy(rows_in, rows_in, recv_sem.at[2]).wait()

    level = lax.broadcasted_iota(jnp.int32, (band, LANES), 1) >> 5
    merged = jnp.zeros((band, LANES), f32)
    for v in range(lev):
        shifted = pltpu.roll(rows_in[pl.ds(v * band, band), :], lax.rem(v - my_lev + lev, lev) * 32, 1)
        merged = jnp.where(level == v, shifted, merged)
    turned = jnp.concatenate([merged, merged], 0).T
    first = lane < band
    sign_a, sign_b = (-1.0, 1.0, -1.0, 1.0), (-1.0, -1.0, 1.0, 1.0)

    def piece_of(v, f):
        return turned[(v * 4 + f) * 8 : (v * 4 + f) * 8 + 8]

    for o in range(4):
        for v in range(lev):
            out_ref[pl.ds((o * lev + v) * 8, 8), :] = jnp.where(
                first, sign_a[o] * piece_of(v, o ^ 1), sign_b[o] * piece_of(v, o ^ 2)
            )
    for load in legendre_loads:
        load.wait()
    pltpu.make_async_copy(request_out.at[pl.ds(0, 4 * (band - 1))], request_out.at[pl.ds(0, 4 * (band - 1))], send_sem.at[0]).wait()
    pltpu.make_async_copy(reply_out.at[pl.ds(0, 2 * (band - 1))], reply_out.at[pl.ds(0, 2 * (band - 1))], send_sem.at[1]).wait()
    sent = rows_in.at[pl.ds(0, lev * band - 1)]
    pltpu.make_async_copy(sent, sent, send_sem.at[2]).wait()


def legendre_kernel(lowest_ref, left_ref, a_ref, b_ref, div_hbm, vort_hbm, div, vort, store_sem):
    owned, _, degrees = a_ref.shape
    half = left_ref.shape[0] // 2
    left = left_ref[...]
    slot = lax.broadcasted_iota(jnp.int32, left.shape, 0) % owned
    pieces = [jnp.where(slot == i, left, 0.0).astype(bf16) for i in range(owned)]
    pieces = [jnp.concatenate(pieces[i : i + 2], 1) for i in range(0, owned, 2)]
    lowest = jnp.concatenate([lowest_ref[...]] * (WIDTH // LANES), 1)
    stores = []
    for j in range(degrees // WIDTH):
        at = pl.ds(j * WIDTH, WIDTH)
        total = jnp.zeros((2 * half, WIDTH), f32)
        for i in range(0, owned, 2):
            right = jnp.concatenate([a_ref[i, :, at], b_ref[i, :, at], a_ref[i + 1, :, at], b_ref[i + 1, :, at]], 0)
            total = total + dot(pieces[i // 2], right)
        keep = j * WIDTH + lax.broadcasted_iota(jnp.int32, (owned, WIDTH), 1) >= lowest
        for r in range(0, half, owned):
            div[r : r + owned, at] = jnp.where(keep, total[r : r + owned], 0.0)
            vort[r : r + owned, at] = jnp.where(keep, total[half + r : half + r + owned], 0.0)
        for k, (source, target) in enumerate(((div, div_hbm), (vort, vort_hbm))):
            stores.append(pltpu.make_async_copy(source.at[:, at], target.at[:, at], store_sem.at[2 * j + k]))
            stores[-1].start()
    for store in stores:
        store.wait()


def local(winds, remap_w, remap_col, block_pick, cycle_ids, wave_ids, legendre_a, legendre_b):
    band, lev = lax.axis_size("band"), lax.axis_size("lev")
    coef, twiddle, inner, outer = tables(band)
    columns = winds.shape[2]
    owned, cycles, degrees = legendre_a.shape
    blocks = columns // BLK
    hbm = pl.BlockSpec(memory_space=pltpu.HBM)
    smem = pl.BlockSpec(memory_space=pltpu.SMEM)
    vmem = pl.BlockSpec(memory_space=pltpu.VMEM)
    left, lowest, leg_a, leg_b = pl.pallas_call(
        functools.partial(modes_kernel, band, lev),
        out_shape=(
            pltpu.VMEM((4 * lev * owned, 2 * cycles), f32),
            pltpu.VMEM((owned, LANES), jnp.int32),
            pltpu.VMEM(legendre_a.shape, bf16),
            pltpu.VMEM(legendre_b.shape, bf16),
        ),
        in_specs=[smem] + [hbm] * 11,
        out_specs=(vmem, vmem, vmem, vmem),
        scratch_shapes=[
            pltpu.VMEM((3 * blocks, BLK), f32),
            pltpu.VMEM((2 * band, LANES), f32),
            pltpu.VMEM((2 * band, LANES), jnp.int32),
            pltpu.VMEM((band, 2 * LANES), jnp.int32),
            pltpu.VMEM((band, LANES), jnp.int32),
            pltpu.SMEM((band, LANES), jnp.int32),
            pltpu.VMEM((M // LANES, LANES), jnp.int32),
            pltpu.VMEM(coef.shape, f32),
            pltpu.VMEM(twiddle.shape, f32),
            pltpu.VMEM(inner.shape, bf16),
            pltpu.VMEM(outer.shape, bf16),
            pltpu.VMEM((blocks, 8, BLK), f32),
            pltpu.VMEM((4 * band, LANES), f32),
            pltpu.VMEM((4 * band, LANES), f32),
            pltpu.VMEM((8 * GROUP, LANES), f32),
            pltpu.VMEM((2 * band, LANES), f32),
            pltpu.VMEM((2 * band, LANES), f32),
            pltpu.VMEM((4 * M // LANES, LANES), f32),
            pltpu.VMEM((band, LANES), f32),
            pltpu.VMEM((lev * band, LANES), f32),
            pltpu.SemaphoreType.DMA((10,)),
            pltpu.SemaphoreType.DMA((3,)),
            pltpu.SemaphoreType.DMA((3,)),
            pltpu.SemaphoreType.DMA((2,)),
        ],
        compiler_params=pltpu.CompilerParams(collective_id=0, has_side_effects=True, vmem_limit_bytes=52 * 2**20),
        name="modes",
    )(
        cycle_ids,
        winds.reshape(3 * blocks, BLK),
        remap_w.reshape(2 * band, LANES),
        remap_col.reshape(2 * band, LANES),
        block_pick,
        wave_ids.reshape(M // LANES, LANES),
        coef,
        twiddle,
        inner,
        outer,
        legendre_a,
        legendre_b,
    )
    shape = jax.ShapeDtypeStruct((2 * lev * owned, degrees), f32)
    divergence, vorticity = pl.pallas_call(
        legendre_kernel,
        out_shape=(shape, shape),
        in_specs=[vmem, vmem, vmem, vmem],
        out_specs=(hbm, hbm),
        scratch_shapes=[
            pltpu.VMEM(shape.shape, f32),
            pltpu.VMEM(shape.shape, f32),
            pltpu.SemaphoreType.DMA((2 * degrees // WIDTH,)),
        ],
        compiler_params=pltpu.CompilerParams(vmem_limit_bytes=32 * 2**20),
        name="legendre",
    )(lowest, left, leg_a, leg_b)
    whole = (2, lev, owned, degrees)
    return divergence.reshape(whole), vorticity.reshape(whole)


def solution(mesh):
    placed = (
        P(None, "lev", "band"),
        P(None, "band", None),
        P(None, "band", None),
        P(),
        P("band"),
        P(),
        P(("band", "lev"), None, None),
        P(("band", "lev"), None, None),
    )
    return jax.shard_map(
        local,
        mesh=mesh,
        in_specs=placed,
        out_specs=(P(None, None, ("band", "lev"), None), P(None, None, ("band", "lev"), None)),
        check_vma=False,
    )
```

```python
import functools
import math

import jax
import jax.numpy as jnp
import numpy as np
from jax import lax
from jax.experimental import pallas as pl
from jax.experimental.pallas import tpu as pltpu
from jax.sharding import PartitionSpec as P

NSIDE = 1024
NPHI = 4096
M = 2048
BLK = 128
PER = 12
TAPS = 4
LANES = 128
GROUP = 8
WIDTH = 512

f32 = jnp.float32
bf16 = jnp.bfloat16


def split(table):
    table = np.asarray(table, np.float32)
    high = table.astype(jnp.bfloat16)
    low = (table - high.astype(np.float32)).astype(jnp.bfloat16)
    return high, low


@functools.cache
def tables(band):
    rho = np.arange(2 * band)
    n = (rho % 2) * band + rho // 2
    b = np.arange(NPHI // (2 * band))
    mu = np.arange(LANES)
    m1 = np.arange(M // LANES)
    turn = 2.0 * np.pi / NPHI
    coef, twiddle, outer_hi, outer_lo = [], [], [], []
    for half in (0, 1):
        delta = 1.0 - 0.5 * half
        azimuth = turn * (2 * band * b[None, :] + n[:, None] + delta)
        zero = np.zeros_like(azimuth)
        cos, sin = np.cos(azimuth), np.sin(azimuth)
        coef.append(np.stack([np.concatenate([-sin, cos, zero, zero], 1), np.concatenate([cos, sin, zero, zero], 1)]))
        phi = turn * mu[None, :] * (n[:, None] + delta)
        twiddle.append(np.stack([np.cos(phi), np.sin(phi)]))
        psi = turn * LANES * m1[:, None] * (n[None, :] + delta)
        full = np.concatenate(
            [np.concatenate([np.cos(psi), np.sin(psi)], 1), np.concatenate([-np.sin(psi), np.cos(psi)], 1)], 0
        )
        high, low = split(full)
        outer_hi.append(high)
        outer_lo.append(low)
    angle = 2.0 * np.pi / b.size * (b[:, None] * mu[None, :])
    inner = np.tile(np.concatenate([np.cos(angle), -np.sin(angle)], 1), (4, 1))
    inner_hi, inner_lo = split(inner)
    return (
        np.stack(coef).astype(np.float32),
        np.stack(twiddle).astype(np.float32),
        np.stack([inner_hi, inner_lo]),
        np.stack([np.stack(outer_hi), np.stack(outer_lo)]),
    )


def dot(a, b):
    return jnp.dot(a, b, preferred_element_type=f32)


def far_first(i, count):
    return count // 2 + (1 - 2 * (i % 2)) * ((i + 1) // 2)


def high_low(x):
    high = x.astype(bf16)
    return high, (x - high.astype(f32)).astype(bf16)


def take(x, index):
    return jnp.take_along_axis(x, index, axis=1, mode="promise_in_bounds")


def modes_kernel(
    band,
    lev,
    cycle_ref,
    winds_hbm,
    weight_hbm,
    column_hbm,
    pick_hbm,
    wave_hbm,
    coef_hbm,
    twiddle_hbm,
    inner_hbm,
    outer_hbm,
    a_hbm,
    b_hbm,
    out_ref,
    lowest_ref,
    leg_a,
    leg_b,
    winds,
    weight,
    column,
    pick_window,
    pick_rows,
    pick,
    wave,
    coef,
    twiddle,
    inner,
    outer,
    table,
    request_out,
    request_in,
    taps,
    reply_out,
    reply_in,
    spectrum,
    rows_out,
    rows_in,
    local_sem,
    send_sem,
    recv_sem,
    legendre_sem,
):
    me = lax.axis_index("band")
    my_lev = lax.axis_index("lev")
    barrier = pltpu.get_barrier_semaphore()

    plane, place = lax.div(me, GROUP), lax.rem(me, GROUP)
    planes = band // GROUP
    places = [lax.rem(place + far_first(k, GROUP), GROUP) for k in range(GROUP)]
    my_levels = [lax.rem(my_lev + far_first(k, lev), lev) for k in range(lev)]

    def each_plane(act):
        def step(k, carry):
            odd = lax.rem(k, 2)
            ahead = planes // 2 + (1 - 2 * odd) * lax.div(k + 1, 2)
            base = lax.rem(plane + ahead, planes) * GROUP
            act(base, [base + p for p in places])
            return carry

        lax.fori_loop(0, planes - 1, step, 0)
        act(plane * GROUP, [plane * GROUP + p for p in places[:-1]])

    def greet(base, others):
        for other in others:
            pl.semaphore_signal(barrier, 1, device_id=(other, my_lev), device_id_type=pl.DeviceIdType.MESH)

    for k in range(planes):
        base = lax.rem(plane + far_first(k, planes), planes) * GROUP
        greet(base, [base + p for p in (places if k < planes - 1 else places[:-1])])
    for i in range(1, lev):
        other = lax.rem(my_lev + i, lev)
        pl.semaphore_signal(barrier, 1, device_id=(me, other), device_id_type=pl.DeviceIdType.MESH)

    window = jnp.minimum(me * PER // LANES, PER * band // LANES - 2)
    pick_at = me * PER - window * LANES
    loads = [
        pltpu.make_async_copy(source, target, local_sem.at[i])
        for i, (source, target) in enumerate(
            (
                (column_hbm, column),
                (weight_hbm, weight),
                (winds_hbm, winds),
                (pick_hbm.at[:, pl.ds(pl.multiple_of(window * LANES, LANES), 2 * LANES)], pick_window),
                (coef_hbm, coef),
                (twiddle_hbm, twiddle),
                (inner_hbm, inner),
                (outer_hbm, outer),
                (wave_hbm, wave),
            )
        )
    ]
    for load in loads:
        load.start()

    def to_band(source, target, other, phase):
        return pltpu.make_async_remote_copy(
            src_ref=source,
            dst_ref=target,
            send_sem=send_sem.at[phase],
            recv_sem=recv_sem.at[phase],
            device_id=(other, my_lev),
            device_id_type=pl.DeviceIdType.MESH,
        )

    loads[0].wait()
    loads[1].wait()
    turned_column = column[...].astype(f32).T
    turned_weight = weight[...].T
    for h in range(2):
        request_out[pl.ds(h, band, stride=4), :] = turned_column[h * band : (h + 1) * band]
        request_out[pl.ds(2 + h, band, stride=4), :] = turned_weight[h * band : (h + 1) * band]
    loads[2].wait()
    blocks = winds.shape[0] // 3
    for a in range(3):
        part = winds[pl.ds(a * blocks, blocks), :]
        table[:, a, :] = part
        table[:, 4 + a, :] = part
    loads[3].wait()
    pick_rows[...] = pltpu.roll(pick_window[...], lax.rem(2 * LANES - pick_at, 2 * LANES), 1)[:, :LANES]
    pick_load = pltpu.make_async_copy(pick_rows, pick, local_sem.at[9])
    pick_load.start()
    pl.semaphore_wait(barrier, band - 1 + lev - 1)
    mine = pltpu.make_async_copy(
        request_out.at[pl.ds(4 * me, 4)], request_in.at[pl.ds(4 * me, 4)], recv_sem.at[0]
    )
    mine.start()

    def send_request(base, others):
        for other in others:
            to_band(request_out.at[pl.ds(4 * other, 4)], request_in.at[pl.ds(4 * me, 4)], other, 0).start()

    each_plane(send_request)
    legendre_loads = [
        pltpu.make_async_copy(a_hbm, leg_a, legendre_sem.at[0]),
        pltpu.make_async_copy(b_hbm, leg_b, legendre_sem.at[1]),
    ]
    for load in legendre_loads:
        load.start()
    sub = lax.broadcasted_iota(jnp.int32, (8, LANES), 0)
    lane = lax.broadcasted_iota(jnp.int32, (8, LANES), 1)
    loads[8].wait()
    slots = out_ref.shape[0] // (4 * lev)
    first_slot = (me * lev + my_lev) * slots
    near = jnp.broadcast_to(wave[pl.ds(lax.div(first_slot, LANES), 1), :], (slots, LANES))
    own = lane == sub + lax.rem(first_slot, LANES)
    lowest_ref[...] = jnp.broadcast_to(jnp.sum(jnp.where(own, near, 0), 1, keepdims=True), (slots, LANES))

    pick_load.wait()
    pltpu.make_async_copy(request_in, request_in, recv_sem.at[0]).wait()

    upper = sub < 4
    group = lane >> 5

    def weigh(other):
        rows = [jnp.broadcast_to(request_in[pl.ds(4 * other + k, 1), :], (8, LANES)) for k in range(4)]
        where = jnp.where(upper, rows[0], rows[1]).astype(jnp.int32)
        scale = jnp.where(upper, rows[2], rows[3])
        within, block = where & (BLK - 1), where >> 7
        total = jnp.zeros((8, LANES), f32)
        for c in range(PER):
            piece = table[pick[other, c]]
            total = jnp.where(block == c, take(piece, within), total)
        return total * scale

    def fold_plane(base, totals):
        for p, total in enumerate(totals):
            taps[pl.ds(8 * p, 8), :] = total
        for r in range(0, 2 * GROUP, 8):
            x, y, z = (taps[pl.ds(4 * r + a, 8, stride=4), :] for a in range(3))
            x, y, z = (u + pltpu.roll(u, 64, 1) for u in (x, y, z))
            x = jnp.where(lane < 64, x, z)
            x, y = (u + pltpu.roll(u, 96, 1) for u in (x, y))
            reply_out[pl.ds(pl.multiple_of(2 * base, 8) + r, 8), :] = jnp.where(group == 1, y, jnp.where(group == 3, 0.0, x))

    def weigh_plane(base):
        return tuple(weigh(base + p) for p in range(GROUP))

    def send_reply(base, others):
        for other in others:
            to_band(reply_out.at[pl.ds(2 * other, 2)], reply_in.at[pl.ds(2 * me, 2)], other, 1).start()

    def base_of(k):
        ahead = planes // 2 + (1 - 2 * lax.rem(k, 2)) * lax.div(k + 1, 2)
        return lax.rem(plane + ahead, planes) * GROUP

    def reply(k, totals):
        following = weigh_plane(base_of(k + 1))
        fold_plane(base_of(k), totals)
        send_reply(base_of(k), [base_of(k) + p for p in places])
        return following

    totals = lax.fori_loop(0, planes - 1, reply, weigh_plane(base_of(0)))
    fold_plane(plane * GROUP, totals)
    send_reply(plane * GROUP, [plane * GROUP + p for p in places[:-1]])
    mine = pltpu.make_async_copy(
        reply_out.at[pl.ds(2 * me, 2)], reply_in.at[pl.ds(2 * me, 2)], recv_sem.at[1]
    )
    mine.start()
    for load in loads[4:8]:
        load.wait()
    pltpu.make_async_copy(reply_in, reply_in, recv_sem.at[1]).wait()

    number = cycle_ref[0]
    odd = (jnp.full((2 * band, LANES), number, jnp.int32) & 1) == 1
    odd_thin = (jnp.full((2 * M // LANES, 4 * band), number, jnp.int32) & 1) == 1

    def by_parity(table, *at):
        return jnp.where(odd, table[(0, *at)], table[(1, *at)])

    cos_theta = 4.0 / 3.0 - 2.0 * jnp.full((2 * band, LANES), number, jnp.int32).astype(f32) / (3.0 * NSIDE)
    sin_theta = jnp.sqrt(1.0 - cos_theta * cos_theta)
    component = lax.broadcasted_iota(jnp.int32, (2 * band, LANES), 1) >> 5
    samples = reply_in[...]
    east = samples * by_parity(coef, 0)
    north = samples * jnp.where(component == 2, sin_theta, -cos_theta * by_parity(coef, 1))
    high, low = high_low(jnp.concatenate([east, north], 0))
    section = dot(high, inner[0]) + dot(low, inner[0]) + dot(high, inner[1])
    cos, sin = by_parity(twiddle, 0), by_parity(twiddle, 1)
    cos, sin = jnp.concatenate([cos, cos], 0), jnp.concatenate([sin, sin], 0)
    real, imag = section[:, :LANES], section[:, LANES:]
    real, imag = real * cos + imag * sin, imag * cos - real * sin
    n = 2 * band
    high, low = high_low(
        jnp.concatenate(
            [jnp.concatenate([real[:n], real[n:]], 1), jnp.concatenate([imag[:n], imag[n:]], 1)], 0
        )
    )
    outer_hi = jnp.where(odd_thin, outer[0, 0], outer[0, 1])
    outer_lo = jnp.where(odd_thin, outer[1, 0], outer[1, 1])
    full = dot(outer_hi, high) + dot(outer_hi, low) + dot(outer_lo, high)
    full = full.astype(bf16).astype(f32)
    rows = M // LANES
    for f, (r, c) in enumerate(((0, 0), (1, 0), (0, 1), (1, 1))):
        spectrum[pl.ds(f * rows, rows), :] = full[r * rows : (r + 1) * rows, c * LANES : (c + 1) * LANES]

    wave_row, wave_lane = wave[...] >> 7, wave[...] & (LANES - 1)
    field = (lane >> 3) & 3
    spot = (lane >> 5) * 8 + (lane & 7)
    for h in range(rows // 8):
        row_of, lane_of = wave_row[8 * h : 8 * h + 8], wave_lane[8 * h : 8 * h + 8]
        ordered = []
        for f in range(4):
            picked = jnp.zeros((8, LANES), f32)
            for r in range(rows):
                source = jnp.broadcast_to(spectrum[pl.ds(f * rows + r, 1), :], (8, LANES))
                picked = jnp.where(row_of == r, take(source, lane_of), picked)
            ordered.append(picked)
        for b in range(4):
            packed = jnp.zeros((8, LANES), f32)
            for f in range(4):
                packed = jnp.where(field == f, take(ordered[f], spot + 32 * b), packed)
            rows_out[pl.ds(32 * h + b, 8, stride=4), :] = packed

    def send_row(other, levels):
        for v in levels:
            pltpu.make_async_remote_copy(
                src_ref=rows_out.at[pl.ds(other, 1)],
                dst_ref=rows_in.at[pl.ds(my_lev * band + me, 1)],
                send_sem=send_sem.at[2],
                recv_sem=recv_sem.at[2],
                device_id=(other, v),
                device_id_type=pl.DeviceIdType.MESH,
            ).start()

    def send_rows(base, others):
        for v in my_levels:
            for other in others:
                send_row(other, [v])

    each_plane(send_rows)
    send_row(me, my_levels[:-1])
    mine = pltpu.make_async_copy(
        rows_out.at[pl.ds(me, 1)], rows_in.at[pl.ds(my_lev * band + me, 1)], recv_sem.at[2]
    )
    mine.start()
    pltpu.make_async_copy(rows_in, rows_in, recv_sem.at[2]).wait()

    level = lax.broadcasted_iota(jnp.int32, (band, LANES), 1) >> 5
    merged = jnp.zeros((band, LANES), f32)
    for v in range(lev):
        shifted = pltpu.roll(rows_in[pl.ds(v * band, band), :], lax.rem(v - my_lev + lev, lev) * 32, 1)
        merged = jnp.where(level == v, shifted, merged)
    turned = jnp.concatenate([merged, merged], 0).T
    first = lane < band
    sign_a, sign_b = (-1.0, 1.0, -1.0, 1.0), (-1.0, -1.0, 1.0, 1.0)

    def piece_of(v, f):
        return turned[(v * 4 + f) * 8 : (v * 4 + f) * 8 + 8]

    for o in range(4):
        for v in range(lev):
            out_ref[pl.ds((o * lev + v) * 8, 8), :] = jnp.where(
                first, sign_a[o] * piece_of(v, o ^ 1), sign_b[o] * piece_of(v, o ^ 2)
            )
    for load in legendre_loads:
        load.wait()
    pltpu.make_async_copy(request_out.at[pl.ds(0, 4 * (band - 1))], request_out.at[pl.ds(0, 4 * (band - 1))], send_sem.at[0]).wait()
    pltpu.make_async_copy(reply_out.at[pl.ds(0, 2 * (band - 1))], reply_out.at[pl.ds(0, 2 * (band - 1))], send_sem.at[1]).wait()
    sent = rows_in.at[pl.ds(0, lev * band - 1)]
    pltpu.make_async_copy(sent, sent, send_sem.at[2]).wait()


def legendre_kernel(lowest_ref, left_ref, a_ref, b_ref, div_hbm, vort_hbm, div, vort, store_sem):
    owned, _, degrees = a_ref.shape
    half = left_ref.shape[0] // 2
    left = left_ref[...]
    slot = lax.broadcasted_iota(jnp.int32, left.shape, 0) % owned
    pieces = [jnp.where(slot == i, left, 0.0).astype(bf16) for i in range(owned)]
    pieces = [jnp.concatenate(pieces[i : i + 2], 1) for i in range(0, owned, 2)]
    lowest = jnp.concatenate([lowest_ref[...]] * (WIDTH // LANES), 1)
    stores = []
    for j in range(degrees // WIDTH):
        at = pl.ds(j * WIDTH, WIDTH)
        total = jnp.zeros((2 * half, WIDTH), f32)
        for i in range(0, owned, 2):
            right = jnp.concatenate([a_ref[i, :, at], b_ref[i, :, at], a_ref[i + 1, :, at], b_ref[i + 1, :, at]], 0)
            total = total + dot(pieces[i // 2], right)
        keep = j * WIDTH + lax.broadcasted_iota(jnp.int32, (owned, WIDTH), 1) >= lowest
        for r in range(0, half, owned):
            div[r : r + owned, at] = jnp.where(keep, total[r : r + owned], 0.0)
            vort[r : r + owned, at] = jnp.where(keep, total[half + r : half + r + owned], 0.0)
        for k, (source, target) in enumerate(((div, div_hbm), (vort, vort_hbm))):
            stores.append(pltpu.make_async_copy(source.at[:, at], target.at[:, at], store_sem.at[2 * j + k]))
            stores[-1].start()
    for store in stores:
        store.wait()


def local(winds, remap_w, remap_col, block_pick, cycle_ids, wave_ids, legendre_a, legendre_b):
    band, lev = lax.axis_size("band"), lax.axis_size("lev")
    coef, twiddle, inner, outer = tables(band)
    columns = winds.shape[2]
    owned, cycles, degrees = legendre_a.shape
    blocks = columns // BLK
    hbm = pl.BlockSpec(memory_space=pltpu.HBM)
    smem = pl.BlockSpec(memory_space=pltpu.SMEM)
    vmem = pl.BlockSpec(memory_space=pltpu.VMEM)
    left, lowest, leg_a, leg_b = pl.pallas_call(
        functools.partial(modes_kernel, band, lev),
        out_shape=(
            pltpu.VMEM((4 * lev * owned, 2 * cycles), f32),
            pltpu.VMEM((owned, LANES), jnp.int32),
            pltpu.VMEM(legendre_a.shape, bf16),
            pltpu.VMEM(legendre_b.shape, bf16),
        ),
        in_specs=[smem] + [hbm] * 11,
        out_specs=(vmem, vmem, vmem, vmem),
        scratch_shapes=[
            pltpu.VMEM((3 * blocks, BLK), f32),
            pltpu.VMEM((2 * band, LANES), f32),
            pltpu.VMEM((2 * band, LANES), jnp.int32),
            pltpu.VMEM((band, 2 * LANES), jnp.int32),
            pltpu.VMEM((band, LANES), jnp.int32),
            pltpu.SMEM((band, LANES), jnp.int32),
            pltpu.VMEM((M // LANES, LANES), jnp.int32),
            pltpu.VMEM(coef.shape, f32),
            pltpu.VMEM(twiddle.shape, f32),
            pltpu.VMEM(inner.shape, bf16),
            pltpu.VMEM(outer.shape, bf16),
            pltpu.VMEM((blocks, 8, BLK), f32),
            pltpu.VMEM((4 * band, LANES), f32),
            pltpu.VMEM((4 * band, LANES), f32),
            pltpu.VMEM((8 * GROUP, LANES), f32),
            pltpu.VMEM((2 * band, LANES), f32),
            pltpu.VMEM((2 * band, LANES), f32),
            pltpu.VMEM((4 * M // LANES, LANES), f32),
            pltpu.VMEM((band, LANES), f32),
            pltpu.VMEM((lev * band, LANES), f32),
            pltpu.SemaphoreType.DMA((10,)),
            pltpu.SemaphoreType.DMA((3,)),
            pltpu.SemaphoreType.DMA((3,)),
            pltpu.SemaphoreType.DMA((2,)),
        ],
        compiler_params=pltpu.CompilerParams(collective_id=0, has_side_effects=True, vmem_limit_bytes=52 * 2**20),
        name="modes",
    )(
        cycle_ids,
        winds.reshape(3 * blocks, BLK),
        remap_w.reshape(2 * band, LANES),
        remap_col.reshape(2 * band, LANES),
        block_pick,
        wave_ids.reshape(M // LANES, LANES),
        coef,
        twiddle,
        inner,
        outer,
        legendre_a,
        legendre_b,
    )
    shape = jax.ShapeDtypeStruct((2 * lev * owned, degrees), f32)
    divergence, vorticity = pl.pallas_call(
        legendre_kernel,
        out_shape=(shape, shape),
        in_specs=[vmem, vmem, vmem, vmem],
        out_specs=(hbm, hbm),
        scratch_shapes=[
            pltpu.VMEM(shape.shape, f32),
            pltpu.VMEM(shape.shape, f32),
            pltpu.SemaphoreType.DMA((2 * degrees // WIDTH,)),
        ],
        compiler_params=pltpu.CompilerParams(vmem_limit_bytes=32 * 2**20),
        name="legendre",
    )(lowest, left, leg_a, leg_b)
    whole = (2, lev, owned, degrees)
    return divergence.reshape(whole), vorticity.reshape(whole)


def solution(mesh):
    placed = (
        P(None, "lev", "band"),
        P(None, "band", None),
        P(None, "band", None),
        P(),
        P("band"),
        P(),
        P(("band", "lev"), None, None),
        P(("band", "lev"), None, None),
    )
    return jax.shard_map(
        local,
        mesh=mesh,
        in_specs=placed,
        out_specs=(P(None, None, ("band", "lev"), None), P(None, None, ("band", "lev"), None)),
        check_vma=False,
    )
```
